256 devices in a mesh: prow: 32 (over z_hi, x, core), pcol: 8 (over z_lo, y).
Axes of the slice: x: 4, y: 4, z: 8 (z_hi: 4, z_lo: 2; z = z_hi * 2 + z_lo), core: 2. Of those that a mesh axis runs over, the one named last changes fastest.
Arguments:
- matrix: float32 [40960, 8192], P('prow', 'pcol'), may hold values from -6 to 6
- pivots: int32 [2, 256], replicated, may hold values from 0 to 40959, as said below
- lower_inverse: float32 [2, 256, 256], replicated, as said below
- upper_inverse: float32 [2, 256, 256], replicated, as said below
Outputs:
- factored: float32 [40960, 8192], P('prow', 'pcol')
The draws below stay inside these ranges and needn't reach their ends.
Inputs may be any that keep to these rules, and one draw needn't show every extreme that they name: `pivots`: the 512 pivot indices are distinct over both steps and none lies in rows k * 1280 to k * 1280 + 255 for k = 0 or 1. `lower_inverse`: unit lower triangular. `upper_inverse`: upper triangular with positive diagonal.
All inputs are finite; a program needn't handle non-finite values.
Results may differ from the reference program's by a relative error of at most 0.0001.
Values sent between devices are 32-bit elements; how exact they have to be, the bound alone decides.
No kernel may reach another device: no remote copies, remote signals or barrier semaphores. Data moves between devices by JAX's collectives and lax.ppermute only.
A program may use at most 64 MiB of HBM per device.

```python
import math
import jax
import jax.numpy as jnp
from jax import lax

NB = 256
COLS_DEV = 1024
ROWS_DEV = 1280
ROWS = 40960
COLS = 8192
N_PROW = 32


def draw_pivots(key, part):
    key = jax.random.fold_in(key, 11)
    key_local, key_pool, key_order = jax.random.split(key, 3)
    half = N_PROW // 2
    forced_dev = jnp.array([[half, 1, N_PROW - 1], [half + 1, 2, 0]], dtype=jnp.int32)
    local = jax.random.randint(key_local, (2, 3), NB, ROWS_DEV).astype(jnp.int32)
    forced = forced_dev * ROWS_DEV + local
    dev_ids = jnp.arange(N_PROW, dtype=jnp.int32)
    is_forced = jnp.any(dev_ids[:, None] == forced_dev.reshape(1, 6), axis=1).astype(jnp.int32)
    others = jnp.argsort(is_forced, stable=True)[:N_PROW - 6].astype(jnp.int32)
    pool = (N_PROW - 6) * ROWS_DEV
    order = jax.random.permutation(key_pool, pool)[:2 * NB - 6].astype(jnp.int32)
    rows = others[order // ROWS_DEV] * ROWS_DEV + order % ROWS_DEV
    combined = jnp.concatenate([forced, rows.reshape(2, NB - 3)], axis=1)
    shuffle = jax.random.permutation(key_order, NB)
    return combined[:, shuffle].astype(jnp.int32)


def draw_lower_inverse(key, part):
    key = jax.random.fold_in(key, 12)
    first = jax.lax.broadcasted_iota(jnp.int32, (2, NB, NB), 1)
    second = jax.lax.broadcasted_iota(jnp.int32, (2, NB, NB), 2)
    values = jax.random.normal(key, (2, NB, NB), jnp.float32)
    below = values * (0.5 / math.sqrt(NB))
    ones = jnp.where(first == second, 1.0, 0.0)
    return jnp.where(first > second, below, ones).astype(jnp.float32)


def draw_upper_inverse(key, part):
    key = jax.random.fold_in(key, 13)
    key_diag, key_off = jax.random.split(key)
    first = jax.lax.broadcasted_iota(jnp.int32, (2, NB, NB), 1)
    second = jax.lax.broadcasted_iota(jnp.int32, (2, NB, NB), 2)
    logs = jax.random.uniform(key_diag, (2, NB, NB), jnp.float32, math.log(1.0 / 64.0), math.log(1.0 / 16.0))
    values = jax.random.normal(key_off, (2, NB, NB), jnp.float32)
    diagonal = jnp.where(first == second, jnp.exp(logs), 0.0)
    return jnp.where(first < second, values / 1024.0, diagonal).astype(jnp.float32)


def block_scale(own_key, dims, cuts, low, high):
    factor_of, own = 1.0, jax.random.fold_in(own_key, 6)
    for dim, shards_of in cuts:
        steps = jnp.exp(jax.random.uniform(jax.random.fold_in(own, dim), (shards_of,), jnp.float32, low / len(cuts), high / len(cuts)))
        factor_of = factor_of * jnp.repeat(steps, dims[dim] // shards_of).reshape([-1 if axis == dim else 1 for axis in range(len(dims))])
    return factor_of


def centred(key, extent, spread, limit, cuts=(), kind=jnp.bfloat16):
    values = spread * jax.random.normal(key, extent, jnp.float32)
    if cuts:
        values = values * block_scale(key, extent, cuts, -0.22, 0.18)
    return jnp.clip(values, -limit, limit).astype(kind)


def setup_inputs(seed: int = 0) -> dict:
    keys = jax.random.split(jax.random.key(seed), 5)
    matrix = centred(keys[0], (ROWS, COLS), 1.0, 6.0, ((0, 32), (1, 8)), jnp.float32)
    pivots = draw_pivots(jax.random.fold_in(keys[4], 71), 0)
    lower_inverse = draw_lower_inverse(jax.random.fold_in(keys[4], 71), 0)
    upper_inverse = draw_upper_inverse(jax.random.fold_in(keys[4], 71), 0)
    return {"matrix": matrix, "pivots": pivots, "lower_inverse": lower_inverse, "upper_inverse": upper_inverse}


def reference(matrix, pivots, lower_inverse, upper_inverse):
    whole = matrix
    row_ids = jnp.arange(ROWS, dtype=jnp.int32)
    col_ids = jnp.arange(COLS, dtype=jnp.int32)
    for step in range(2):
        targets = pivots[step]
        top_start = step * ROWS_DEV
        panel_start = step * COLS_DEV
        new_top = whole[targets]
        old_top = whole[top_start:top_start + NB]
        whole = whole.at[targets].set(old_top)
        whole = whole.at[top_start:top_start + NB].set(new_top)
        row_keep = jnp.logical_not((row_ids // ROWS_DEV <= step) & (row_ids % ROWS_DEV < NB))
        col_keep = jnp.logical_not((col_ids // COLS_DEV <= step) & (col_ids % COLS_DEV < NB))
        panel = whole[:, panel_start:panel_start + NB]
        lfactor = jnp.dot(panel, upper_inverse[step], precision=lax.Precision.HIGHEST, preferred_element_type=jnp.float32)
        lfactor = jnp.where(row_keep[:, None], lfactor, 0.0)
        ufull = jnp.dot(lower_inverse[step], new_top, precision=lax.Precision.HIGHEST, preferred_element_type=jnp.float32)
        ufactor = jnp.where(col_keep[None, :], ufull, 0.0)

        def update(pair):
            block, left = pair
            return block - jnp.dot(left, ufactor, precision=lax.Precision.HIGHEST, preferred_element_type=jnp.float32)

        whole = lax.map(update, (whole.reshape(N_PROW, ROWS_DEV, COLS), lfactor.reshape(N_PROW, ROWS_DEV, NB))).reshape(ROWS, COLS)
        old_panel = whole[:, panel_start:panel_start + NB]
        whole = whole.at[:, panel_start:panel_start + NB].set(jnp.where(row_keep[:, None], lfactor, old_panel))
        old_rows = whole[top_start:top_start + NB]
        whole = whole.at[top_start:top_start + NB].set(jnp.where(col_keep[None, :], ufull, old_rows))
    return whole
```

```python
import functools

import jax
import jax.numpy as jnp
from jax import lax
from jax.experimental import pallas as pl
from jax.experimental.pallas import tpu as pltpu
from jax.sharding import PartitionSpec as P

NB = 256
ROWS_DEV = 1280
COLS_DEV = 1024
XS = 4
ZS = 4
QUARTER = NB // XS
SUB = QUARTER // ZS
EXT = COLS_DEV + NB + COLS_DEV + 2 * NB
BLOCK = 256
VMEM_LIMIT = 50 * 1024 * 1024


def shift(core, x, z):
    pairs = []
    for index in range(2 * XS * ZS):
        c, xi, zi = index % 2, index // 2 % XS, index // (2 * XS)
        target = ((zi + z) % ZS * XS + (xi + x) % XS) * 2 + (c + core) % 2
        pairs.append((index, target))
    return pairs


def send(value, core=0, x=0, z=0):
    return lax.ppermute(value, "prow", shift(core, x, z))


def send_from(value, keep, core=0, x=0, z=0):
    pairs = [pair for pair in shift(core, x, z) if keep(pair[0] // 2 % XS, pair[0] // (2 * XS))]
    return lax.ppermute(value, "prow", pairs)


def pick_kernel(place, pivots, a_ref, mine, theirs, rows, sources, count):
    prow, x, z, core = place[0], place[1], place[2], place[3]
    offset = prow * ROWS_DEV
    mine[...] = jnp.zeros_like(mine)
    theirs[...] = jnp.zeros_like(theirs)
    count[0] = 0
    for step in range(2):
        own = core == step

        def body(i, carry):
            local = pivots[step, i] - offset

            @pl.when((local >= 0) & (local < ROWS_DEV))
            def _():
                quarter, sub, low = i // QUARTER, i // SUB % ZS, i % SUB
                dest = (quarter - x + XS) % XS * QUARTER + (sub - z + ZS) % ZS * SUB + low
                where = (x - quarter + XS) % XS * QUARTER + (z - sub + ZS) % ZS * SUB + low
                n = count[0]
                rows[n] = local
                sources[n] = where + jnp.where(own, 0, NB)
                count[0] = n + 1
                row = a_ref[pl.ds(local, 1), :]

                @pl.when(own)
                def _():
                    mine[pl.ds(dest, 1), :] = row

                @pl.when(jnp.logical_not(own))
                def _():
                    theirs[pl.ds(dest, 1), :] = row

            return carry

        lax.fori_loop(0, NB, body, 0, unroll=8)


def pick(place, pivots, matrix):
    smem = pl.BlockSpec(memory_space=pltpu.SMEM)
    vmem = pl.BlockSpec(memory_space=pltpu.VMEM)
    half = jax.ShapeDtypeStruct((NB, COLS_DEV), jnp.float32)
    entries = jax.ShapeDtypeStruct((2 * NB,), jnp.int32)
    return pl.pallas_call(
        pick_kernel,
        out_shape=[half, half, entries, entries, jax.ShapeDtypeStruct((1,), jnp.int32)],
        in_specs=[smem, smem, vmem],
        out_specs=[vmem, vmem, smem, smem, smem],
        compiler_params=pltpu.CompilerParams(vmem_limit_bytes=VMEM_LIMIT),
        name="pick_rows",
    )(place, pivots, matrix)


def split(value):
    high = value.astype(jnp.bfloat16)
    low = (value - high.astype(jnp.float32)).astype(jnp.bfloat16)
    return high, low


def mul(a, b):
    dot = functools.partial(jnp.dot, preferred_element_type=jnp.float32)
    return dot(a[0], b[0]) + (dot(a[0], b[1]) + dot(a[1], b[0]))


def update_kernel(
    place, rows, sources, count, a_ref, p_ref, g0_ref, g1_ref, m_ref, w_ref, out_ref,
    xs, uh, ul, top, ph, wh, wl, ch, cl,
):
    prow, x, z, core, pcol = place[0], place[1], place[2], place[3], place[4]
    block = pl.program_id(0)

    @pl.when(block == 0)
    def _():
        for part, g_ref in ((0, g0_ref), (1, g1_ref)):
            step = core if part == 0 else 1 - core
            for j in range(XS):
                for k in range(ZS):
                    dest = step * NB + (x - j + XS) % XS * QUARTER + (z - k + ZS) % ZS * SUB
                    dest = pl.multiple_of(dest, SUB)
                    src = j * QUARTER + k * SUB
                    xs[pl.ds(dest, SUB), :] = g_ref[src:src + SUB, : COLS_DEV + NB]
        w0, w1 = split(w_ref[0]), split(w_ref[1])
        wh[0], wl[0] = w0
        wh[1], wl[1] = w1
        m0, m1 = split(m_ref[0]), split(m_ref[1])
        l0r1 = mul(split(xs[NB:, COLS_DEV:]), w0)
        u0c1 = mul(m0, split(xs[:NB, COLS_DEV:]))
        ch[...], cl[...] = split(u0c1)
        l0r1s = split(l0r1)
        for n in range(COLS_DEV // NB):
            cols = slice(n * NB, (n + 1) * NB)
            x0 = xs[:NB, cols]
            u0 = mul(m0, split(x0))
            u0s = split(u0)
            y1 = xs[NB:, cols] - mul(l0r1s, u0s)
            u1 = mul(m1, split(y1))
            u1s = split(u1)
            uh[:NB, cols], ul[:NB, cols] = u0s
            uh[NB:, cols], ul[NB:, cols] = u1s
            if n == 0:
                u0 = jnp.where(pcol == 0, x0, u0)
                u1 = jnp.where(pcol == 0, l0r1, jnp.where(pcol == 1, y1, u1))
            top[:, cols] = jnp.where(prow == 0, u0, u1)

    @pl.when((block == 0) & (prow < 2))
    def _():
        out_ref[...] = top[...]

    @pl.when((block > 0) | (prow >= 2))
    def _():
        out_ref[...] = a_ref[...]
        ph[...] = p_ref[...]
        base = block * BLOCK

        def patch(n, carry):
            local = rows[n] - base

            @pl.when((local >= 0) & (local < BLOCK))
            def _():
                src = sources[n]

                @pl.when(src < NB)
                def _():
                    row = g0_ref[pl.ds(src, 1), COLS_DEV + NB:]
                    out_ref[pl.ds(local, 1), :] = row[:, :COLS_DEV]
                    ph[pl.ds(local, 1), :] = row[:, COLS_DEV:]

                @pl.when(src >= NB)
                def _():
                    row = g1_ref[pl.ds(src - NB, 1), COLS_DEV + NB:]
                    out_ref[pl.ds(local, 1), :] = row[:, :COLS_DEV]
                    ph[pl.ds(local, 1), :] = row[:, COLS_DEV:]

            return carry

        lax.fori_loop(0, count[0], patch, 0)
        w0, w1 = (wh[0], wl[0]), (wh[1], wl[1])
        l0 = mul(split(ph[:, :NB]), w0)
        l0s = split(l0)
        l1 = mul(split(ph[:, NB:] - mul(l0s, (ch[...], cl[...]))), w1)
        l1s = split(l1)
        ls = tuple(jnp.concatenate([a, b], axis=1) for a, b in zip(l0s, l1s))
        for n in range(COLS_DEV // NB):
            cols = slice(n * NB, (n + 1) * NB)
            out_ref[:, cols] = out_ref[:, cols] - mul(ls, (uh[:, cols], ul[:, cols]))

        @pl.when(pcol == 0)
        def _():
            out_ref[:, :NB] = l0

        @pl.when(pcol == 1)
        def _():
            out_ref[:, :NB] = l1


def update(place, rows, sources, count, matrix, panels, g0, g1, lower, upper):
    smem = pl.BlockSpec(memory_space=pltpu.SMEM)
    vmem = pl.BlockSpec(memory_space=pltpu.VMEM)
    f32, bf16 = jnp.float32, jnp.bfloat16
    return pl.pallas_call(
        update_kernel,
        grid=(ROWS_DEV // BLOCK,),
        out_shape=jax.ShapeDtypeStruct((ROWS_DEV, COLS_DEV), f32),
        in_specs=[
            smem, smem, smem, smem,
            pl.BlockSpec((BLOCK, COLS_DEV), lambda i: (i, 0)),
            pl.BlockSpec((BLOCK, 2 * NB), lambda i: (i, 0)),
            vmem, vmem, vmem, vmem,
        ],
        out_specs=pl.BlockSpec((BLOCK, COLS_DEV), lambda i: (i, 0)),
        scratch_shapes=[
            pltpu.VMEM((2 * NB, COLS_DEV + NB), f32),
            pltpu.VMEM((2 * NB, COLS_DEV), bf16),
            pltpu.VMEM((2 * NB, COLS_DEV), bf16),
            pltpu.VMEM((NB, COLS_DEV), f32),
            pltpu.VMEM((BLOCK, 2 * NB), f32),
            pltpu.VMEM((2, NB, NB), bf16),
            pltpu.VMEM((2, NB, NB), bf16),
            pltpu.VMEM((NB, NB), bf16),
            pltpu.VMEM((NB, NB), bf16),
        ],
        compiler_params=pltpu.CompilerParams(vmem_limit_bytes=VMEM_LIMIT),
        name="panel_update",
    )(place, rows, sources, count, matrix, panels, g0, g1, lower, upper)


def on_device(matrix, pivots, lower_inverse, upper_inverse):
    prow, pcol = lax.axis_index("prow"), lax.axis_index("pcol")
    core, x, z = prow % 2, prow // 2 % XS, prow // (2 * XS)
    place = jnp.stack([prow, x, z, core, pcol]).astype(jnp.int32)

    scattered = lax.all_to_all(matrix[:, :NB], "pcol", 0, 0, tiled=True)
    part = ROWS_DEV // 8
    panels = jnp.concatenate([scattered[:part], scattered[part:2 * part]], axis=1)
    panels = lax.all_gather(panels, "pcol", tiled=True)

    mine, theirs, rows, sources, count = pick(place, pivots, matrix)
    total = (mine + send(theirs, core=1)).reshape(XS, QUARTER, COLS_DEV)
    total = total[0] + sum(send(total[j], x=j) for j in range(1, XS))
    total = total.reshape(ZS, SUB, COLS_DEV)
    total = total[0] + sum(send(total[k], z=k) for k in range(1, ZS))

    top = matrix[:NB].reshape(XS, QUARTER, COLS_DEV)
    spread = sum(
        send_from(top[j], lambda xi, zi: xi == 0 and zi == 0, x=j) for j in range(1, XS)
    )
    quarter = jnp.where(x == 0, top[0], spread).reshape(ZS, SUB, COLS_DEV)
    spread = sum(send_from(quarter[k], lambda xi, zi: zi == 0, z=k) for k in range(1, ZS))
    displaced = jnp.where(z == 0, quarter[0], spread)

    extra = jnp.concatenate([total[:, :NB], displaced[:, :NB]], axis=0)
    extra = lax.all_to_all(jnp.tile(extra, (8, 1)), "pcol", 0, 0, tiled=True)
    from_0, from_1 = extra[:2 * SUB], extra[2 * SUB:4 * SUB]
    crossed = jnp.where(core == 0, from_1[:SUB], from_0[:SUB])
    held = jnp.concatenate([total, crossed, displaced, from_0[SUB:], from_1[SUB:]], axis=1)

    held = jnp.concatenate([held] + [send(held, z=k) for k in range(1, ZS)], axis=0)
    held = jnp.concatenate([held] + [send(held, x=j) for j in range(1, XS)], axis=0)
    other = send(held, core=1)
    return update(
        place, rows, sources, count, matrix, panels, held, other, lower_inverse, upper_inverse
    )


def solution(mesh):
    in_specs = (P("prow", "pcol"), P(), P(), P())
    out_specs = P("prow", "pcol")
    return jax.shard_map(
        on_device, mesh=mesh, in_specs=in_specs, out_specs=out_specs, check_vma=False
    )
```

```python
import functools

import jax
import jax.numpy as jnp
from jax import lax
from jax.experimental import pallas as pl
from jax.experimental.pallas import tpu as pltpu
from jax.sharding import PartitionSpec as P

NB = 256
ROWS_DEV = 1280
COLS_DEV = 1024
XS = 4
ZS = 4
QUARTER = NB // XS
SUB = QUARTER // ZS
BLOCK = 256
PART = ROWS_DEV // 8
HALF = 32


def shift(core, x, z):
    pairs = []
    for index in range(2 * XS * ZS):
        c, xi, zi = index % 2, index // 2 % XS, index // (2 * XS)
        target = ((zi + z) % ZS * XS + (xi + x) % XS) * 2 + (c + core) % 2
        pairs.append((index, target))
    return pairs


def send(value, core=0, x=0, z=0):
    return lax.ppermute(value, "prow", shift(core, x, z))


def send_from(value, keep, core=0, x=0, z=0):
    pairs = [pair for pair in shift(core, x, z) if keep(pair[0] // 2 % XS, pair[0] // (2 * XS))]
    return lax.ppermute(value, "prow", pairs)


def owned_rows(pivots, prow, number):
    local = pivots.reshape(2 * NB) - prow * ROWS_DEV
    owned = (local >= 0) & (local < ROWS_DEV)
    index = lax.broadcasted_iota(jnp.int32, (2 * NB, 2 * NB), 0)
    other = lax.broadcasted_iota(jnp.int32, (2 * NB, 2 * NB), 1)
    before = jnp.sum(jnp.where(owned[None, :] & (other < index), 1, 0), axis=1)
    slot = jnp.where(owned, before, 2 * NB)
    packed = local * (2 * NB) + number
    entries = jnp.sum(jnp.where(slot[None, :] == index, packed[None, :], 0), axis=1)
    return entries, jnp.sum(jnp.where(owned, 1, 0)).reshape(1)


def pick_kernel(place, entries, count, a_ref, mine, theirs, panel, top, sem, panel_sem, top_sem):
    x, z, core = place[1], place[2], place[3]
    panel_copy = pltpu.make_async_copy(a_ref.at[:, :NB], panel, panel_sem)
    top_copy = pltpu.make_async_copy(a_ref.at[:NB, :], top, top_sem)
    panel_copy.start()
    top_copy.start()
    mine[...] = jnp.zeros_like(mine)
    theirs[...] = jnp.zeros_like(theirs)

    def start(n, carry):
        local, number = entries[n] // (2 * NB), entries[n] % (2 * NB)
        i = number % NB
        quarter, sub, low = i // QUARTER, i // SUB % ZS, i % SUB
        dest = (quarter - x + XS) % XS * QUARTER + (sub - z + ZS) % ZS * SUB + low
        own = core == number // NB
        row = a_ref.at[pl.ds(local, 1), :]

        @pl.when(own)
        def _():
            pltpu.make_async_copy(row, mine.at[pl.ds(dest, 1), :], sem).start()

        @pl.when(jnp.logical_not(own))
        def _():
            pltpu.make_async_copy(row, theirs.at[pl.ds(dest, 1), :], sem).start()

        return carry

    def wait(n, carry):
        pltpu.make_async_copy(a_ref.at[pl.ds(0, 1), :], mine.at[pl.ds(0, 1), :], sem).wait()
        return carry

    lax.fori_loop(0, count[0], start, 0)
    lax.fori_loop(0, count[0], wait, 0)
    panel_copy.wait()
    top_copy.wait()


def pick(place, entries, count, matrix):
    smem = pl.BlockSpec(memory_space=pltpu.SMEM)
    vmem = pl.BlockSpec(memory_space=pltpu.VMEM)
    half = jax.ShapeDtypeStruct((NB, COLS_DEV), jnp.float32)
    return pl.pallas_call(
        pick_kernel,
        out_shape=[half, half, jax.ShapeDtypeStruct((ROWS_DEV, NB), jnp.float32), half],
        in_specs=[smem, smem, smem, pl.BlockSpec(memory_space=pltpu.HBM)],
        out_specs=[vmem] * 4,
        scratch_shapes=[pltpu.SemaphoreType.DMA] * 3,
        compiler_params=pltpu.CompilerParams(vmem_limit_bytes=8 * 1024 * 1024),
        name="pick_rows",
    )(place, entries, count, matrix)


def split(value):
    high = value.astype(jnp.bfloat16)
    low = (value - high.astype(jnp.float32)).astype(jnp.bfloat16)
    return high, low


def mul(a, b):
    dot = functools.partial(jnp.dot, preferred_element_type=jnp.float32)
    return dot(a[0], b[0]) + (dot(a[0], b[1]) + dot(a[1], b[0]))


def three(value):
    high, rest = value.astype(jnp.bfloat16), None
    rest = value - high.astype(jnp.float32)
    middle = rest.astype(jnp.bfloat16)
    return high, middle, (rest - middle.astype(jnp.float32)).astype(jnp.bfloat16)


def spread_kernel(place, own_ref, other_ref, pick_own, pick_other, *refs):
    outs = refs[-XS:]

    @pl.when((place[1] == 0) & (place[2] == 0))
    def _():
        rows = ZS * HALF
        for n in range(COLS_DEV // NB):
            cols = slice(n * NB, (n + 1) * NB)
            own, other = three(own_ref[:, cols]), three(other_ref[:, cols])
            for j in range(XS):
                block = slice(j * rows, (j + 1) * rows)
                dot = functools.partial(jnp.dot, preferred_element_type=jnp.float32)
                total = [
                    dot(pick_own[block, :], a) + dot(pick_other[block, :], b)
                    for a, b in zip(own, other)
                ]
                outs[j][:, cols] = total[0] + (total[1] + total[2])


def spread(place, own, other, picks, tokens):
    smem, vmem = pl.BlockSpec(memory_space=pltpu.SMEM), pl.BlockSpec(memory_space=pltpu.VMEM)
    anywhere = pl.BlockSpec(memory_space=pl.ANY)
    shape = jax.ShapeDtypeStruct((ZS * HALF, COLS_DEV), jnp.float32)
    return pl.pallas_call(
        spread_kernel,
        out_shape=[shape] * XS,
        in_specs=[smem, vmem, vmem, vmem, vmem] + [anywhere] * len(tokens),
        out_specs=[vmem] * XS,
        compiler_params=pltpu.CompilerParams(vmem_limit_bytes=16 * 1024 * 1024),
        name="spread_rows",
    )(place, own, other, *picks, *tokens)


def choose_kernel(axis, tokens, place, *refs):
    pieces, outs = refs[:4], refs[4 + tokens:]
    rows = outs[0].shape[0]
    for n, piece in enumerate(pieces):

        @pl.when(place[axis] == n)
        def _():
            for i, out in enumerate(outs):
                out[...] = piece[i * rows:(i + 1) * rows, :]


def choose(place, axis, pieces, count, tokens):
    smem, vmem = pl.BlockSpec(memory_space=pltpu.SMEM), pl.BlockSpec(memory_space=pltpu.VMEM)
    anywhere = pl.BlockSpec(memory_space=pl.ANY)
    rows, cols = pieces[0].shape
    return pl.pallas_call(
        functools.partial(choose_kernel, axis, len(tokens)),
        out_shape=[jax.ShapeDtypeStruct((rows // count, cols), jnp.float32)] * count,
        in_specs=[smem] + [vmem] * 4 + [anywhere] * len(tokens),
        out_specs=[vmem] * count,
        compiler_params=pltpu.CompilerParams(vmem_limit_bytes=8 * 1024 * 1024),
        name="choose_piece",
    )(place, *pieces, *tokens)


def update_kernel(
    packed, place, entries, count, a_ref, p_ref, m_ref, w_ref, *refs
):
    pieces, displaced = refs[:2 * XS], refs[2 * XS:-10]
    out_ref, xs, uh, ul, top, ph, wh, wl, ch, cl = refs[-10:]
    prow, x, z, core, pcol = place[0], place[1], place[2], place[3], place[4]
    block = pl.program_id(0)

    @pl.when(block == 0)
    def _():
        for piece in range(2 * XS):
            step = core if piece < XS else 1 - core
            for k in range(ZS):
                dest = step * NB + (x - piece + 2 * XS) % XS * QUARTER + (z - k + ZS) % ZS * SUB
                dest = pl.multiple_of(dest, SUB)
                xs[pl.ds(dest, SUB), :] = pieces[piece][k * SUB:(k + 1) * SUB, :]
        w0, w1 = split(w_ref[0]), split(w_ref[1])
        wh[0], wl[0] = w0
        wh[1], wl[1] = w1
        m0, m1 = split(m_ref[0]), split(m_ref[1])
        l0r1 = mul(split(xs[NB:, COLS_DEV:]), w0)
        u0c1 = mul(m0, split(xs[:NB, COLS_DEV:]))
        ch[...], cl[...] = split(u0c1)
        l0r1s = split(l0r1)
        u0 = mul(m0, split(xs[:NB, :COLS_DEV]))
        u0s = split(u0)
        uh[:NB, :], ul[:NB, :] = u0s
        y1 = xs[NB:, :COLS_DEV] - mul(l0r1s, u0s)
        u1 = mul(m1, split(y1))
        uh[NB:, :], ul[NB:, :] = split(u1)

        @pl.when(prow == 0)
        def _():
            top[...] = u0

            @pl.when(pcol == 0)
            def _():
                top[:, :NB] = xs[:NB, :NB]

        @pl.when(prow == 1)
        def _():
            top[...] = u1

            @pl.when(pcol == 0)
            def _():
                top[:, :NB] = l0r1

            @pl.when(pcol == 1)
            def _():
                top[:, :NB] = y1[:, :NB]

    @pl.when((block == 0) & (prow < 2))
    def _():
        out_ref[...] = top[...]

    @pl.when((block > 0) | (prow >= 2))
    def _():
        out_ref[...] = a_ref[...]
        ph[...] = p_ref[...]
        base = block * BLOCK

        def patch(n, carry):
            local, number = entries[n] // (2 * NB) - base, entries[n] % (2 * NB)

            @pl.when((local >= 0) & (local < BLOCK))
            def _():
                if packed:
                    src = number % HALF
                    piece = jnp.where(core == number // HALF, 0, 1)
                else:
                    i = number % NB
                    src = (z - i // SUB % ZS + ZS) % ZS * SUB + i % SUB
                    piece = jnp.where(core == number // NB, 0, XS) + (x - i // QUARTER + XS) % XS
                for j in range(len(displaced)):

                    @pl.when(piece == j)
                    def _():
                        row = displaced[j][pl.ds(src, 1), :]
                        out_ref[pl.ds(local, 1), :] = row[:, :COLS_DEV]
                        ph[pl.ds(local, 1), :] = row[:, COLS_DEV:]

            return carry

        lax.fori_loop(0, count[0], patch, 0)
        w0, w1 = (wh[0], wl[0]), (wh[1], wl[1])
        l0 = mul(split(ph[:, :NB]), w0)
        l0s = split(l0)
        l1 = mul(split(ph[:, NB:] - mul(l0s, (ch[...], cl[...]))), w1)
        l1s = split(l1)
        ls = tuple(jnp.concatenate([a, b], axis=1) for a, b in zip(l0s, l1s))
        for n in range(COLS_DEV // NB):
            cols = slice(n * NB, (n + 1) * NB)
            out_ref[:, cols] = out_ref[:, cols] - mul(ls, (uh[:, cols], ul[:, cols]))

        @pl.when(pcol == 0)
        def _():
            out_ref[:, :NB] = l0

        @pl.when(pcol == 1)
        def _():
            out_ref[:, :NB] = l1


def update(packed, place, entries, count, matrix, panels, lower, upper, pieces, displaced):
    smem = pl.BlockSpec(memory_space=pltpu.SMEM)
    vmem = pl.BlockSpec(memory_space=pltpu.VMEM)
    f32, bf16 = jnp.float32, jnp.bfloat16
    wide = pl.BlockSpec((BLOCK, COLS_DEV), lambda i: (i, 0))
    return pl.pallas_call(
        functools.partial(update_kernel, packed),
        grid=(ROWS_DEV // BLOCK,),
        out_shape=jax.ShapeDtypeStruct((ROWS_DEV, COLS_DEV), f32),
        in_specs=[smem, smem, smem, wide, pl.BlockSpec((BLOCK, 2 * NB), lambda i: (i, 0))]
        + [vmem] * (2 + len(pieces) + len(displaced)),
        out_specs=wide,
        scratch_shapes=[
            pltpu.VMEM((2 * NB, COLS_DEV + NB), f32),
            pltpu.VMEM((2 * NB, COLS_DEV), bf16),
            pltpu.VMEM((2 * NB, COLS_DEV), bf16),
            pltpu.VMEM((NB, COLS_DEV), f32),
            pltpu.VMEM((BLOCK, 2 * NB), f32),
            pltpu.VMEM((2, NB, NB), bf16),
            pltpu.VMEM((2, NB, NB), bf16),
            pltpu.VMEM((NB, NB), bf16),
            pltpu.VMEM((NB, NB), bf16),
        ],
        compiler_params=pltpu.CompilerParams(vmem_limit_bytes=40 * 1024 * 1024),
        name="panel_update",
    )(place, entries, count, matrix, panels, lower, upper, *pieces, *displaced)


def add_kernel(n, tokens, *refs):
    parts, outs = refs[:n], refs[n + tokens:]
    rows = outs[0].shape[0]
    for i, out in enumerate(outs):
        block = slice(i * rows, (i + 1) * rows)
        value = parts[0][block, :]
        for part in parts[1:]:
            value = value + part[block, :]
        out[...] = value


def add(parts, count, tokens=()):
    vmem, anywhere = pl.BlockSpec(memory_space=pltpu.VMEM), pl.BlockSpec(memory_space=pl.ANY)
    rows, cols = parts[0].shape
    return pl.pallas_call(
        functools.partial(add_kernel, len(parts), len(tokens)),
        out_shape=[jax.ShapeDtypeStruct((rows // count, cols), jnp.float32)] * count,
        in_specs=[vmem] * len(parts) + [anywhere] * len(tokens),
        out_specs=[vmem] * count,
        compiler_params=pltpu.CompilerParams(vmem_limit_bytes=8 * 1024 * 1024),
        name="add_parts",
    )(*parts, *tokens)


def sync(*values):
    anywhere = pl.BlockSpec(memory_space=pl.ANY)
    return pl.pallas_call(
        lambda *refs: None,
        out_shape=[jax.ShapeDtypeStruct(value.shape, value.dtype) for value in values],
        in_specs=[anywhere] * len(values),
        out_specs=[anywhere] * len(values),
        input_output_aliases={i: i for i in range(len(values))},
        compiler_params=pltpu.CompilerParams(vmem_limit_bytes=1024 * 1024),
        name="sync",
    )(*values)


def pack_kernel(groups, count, *refs):
    parts, out = refs[:groups * count], refs[-1]
    col = 0
    for i in range(groups):
        rows, width = parts[i * count].shape
        for k in range(count):
            out[k * rows:(k + 1) * rows, col:col + width] = parts[i * count + k][...]
        col += width


def pack(groups, tokens=()):
    vmem, anywhere = pl.BlockSpec(memory_space=pltpu.VMEM), pl.BlockSpec(memory_space=pl.ANY)
    cols = sum(group[0].shape[1] for group in groups)
    parts = [part for group in groups for part in group]
    return pl.pallas_call(
        functools.partial(pack_kernel, len(groups), len(groups[0])),
        out_shape=jax.ShapeDtypeStruct((groups[0][0].shape[0] * len(groups[0]), cols), jnp.float32),
        in_specs=[vmem] * len(parts) + [anywhere] * len(tokens),
        out_specs=vmem,
        compiler_params=pltpu.CompilerParams(vmem_limit_bytes=8 * 1024 * 1024),
        name="pack_blocks",
    )(*parts, *tokens)


def gather_z(held):
    return [held] + [send(held, z=k) for k in range(1, ZS)]


def gather_x(held):
    pieces = [held] + [send(held, x=j) for j in range(1, XS)]
    return pieces + [send(piece, core=1) for piece in pieces]


def to_columns(value):
    rows = value.shape[0]
    value = lax.all_to_all(jnp.tile(value, (8, 1)), "pcol", 0, 0, tiled=True)
    return value[:rows], value[rows:2 * rows]


def panel_parts(panel):
    parts = lax.all_to_all(panel, "pcol", 0, 0, tiled=True)
    return jnp.concatenate([parts[:PART], parts[PART:2 * PART]], axis=1)


def panel_rows(parts):
    return lax.all_to_all(jnp.tile(parts, (8, 1)), "pcol", 0, 0, tiled=True)


def from_root(pieces, axis):
    keep = (lambda xi, zi: xi == 0 and zi == 0) if axis == "x" else (lambda xi, zi: zi == 0)
    return [pieces[0]] + [send_from(pieces[n], keep, **{axis: n}) for n in range(1, 4)]


def on_device(matrix, pivots, lower_inverse, upper_inverse):
    prow = lax.axis_index("prow")
    core, x, z = prow % 2, prow // 2 % XS, prow // (2 * XS)
    place = jnp.stack([prow, x, z, core, lax.axis_index("pcol")]).astype(jnp.int32)
    operands = (place, matrix, pivots, lower_inverse, upper_inverse)
    result, most = exchange(True, *operands)
    return lax.while_loop(
        lambda state: state[0],
        lambda state: (False, exchange(False, *operands)[0]),
        (most >= 2 * HALF, result),
    )[1]


def chip_places(pivots):
    number = lax.broadcasted_iota(jnp.int32, (2 * NB,), 0)
    chip = pivots.reshape(2 * NB) // (2 * ROWS_DEV)
    before = number[None, :] < number[:, None]
    return chip, jnp.sum(jnp.where(before & (chip[None, :] == chip[:, None]), 1, 0), axis=1)


def exchange(packed, place, matrix, pivots, lower_inverse, upper_inverse):
    prow, core = place[0], place[3]

    number = lax.broadcasted_iota(jnp.int32, (2 * NB,), 0)
    entries, count = owned_rows(pivots, prow, number)
    mine, theirs, panel, top = pick(place, entries, count, matrix)
    parts = panel_parts(panel)
    theirs, pivots = sync(theirs, pivots)
    chip, rank = chip_places(pivots)
    summed = add([mine, send(theirs, core=1)], XS)
    received = [send(summed[j], x=j) for j in range(1, XS)]

    if packed:
        other = send_from(top, lambda xi, zi: xi == 0 and zi == 0, core=1)
        where = (chip % XS * ZS + chip // XS) * HALF + rank % HALF
        where = jnp.where(rank // HALF == core, where, -1).reshape(2, 1, NB)
        index = lax.broadcasted_iota(jnp.int32, (XS * ZS * HALF, NB), 0)
        steps = [jnp.where(core == 0, where[k], where[1 - k]) for k in range(2)]
        picks = [(index == step).astype(jnp.bfloat16) for step in steps]
        quarters = spread(place, top, other, picks, summed[:1])
    else:
        quarters = add([top], XS)
    total = add([summed[0]] + received, ZS)
    *total, parts = sync(*total, parts)

    panels = panel_rows(parts)
    received = [send(total[k], z=k) for k in range(1, ZS)]
    total, *quarters = sync(add([total[0]] + received, 1)[0], *quarters)

    blocks = gather_z(total)
    panels, columns = sync(panels, total[:, :NB])
    from_0, from_1 = to_columns(columns)
    crossed = jnp.where(core == 0, from_1, from_0)
    subs = choose(place, 1, from_root(quarters, "x"), ZS, [])
    values = sync(*blocks, crossed, *subs)
    blocks, crossed, subs = values[:ZS], values[ZS], values[ZS + 1:]

    (displaced,) = choose(place, 2, from_root(subs, "z"), 1, [])
    total, displaced = sync(pack([blocks, gather_z(crossed)]), displaced)

    total = gather_x(total)
    columns = [[part] for part in to_columns(displaced[:, :NB])]
    displaced = pack([[displaced]] + columns)
    if packed:
        entries, _ = owned_rows(pivots, prow, rank)
        displaced = [displaced, send(displaced, core=1)]
    else:
        displaced = gather_x(pack([gather_z(displaced)]))
    result = update(
        packed, place, entries, count, matrix, panels, lower_inverse, upper_inverse,
        total, displaced,
    )
    return result, jnp.max(rank)


def solution(mesh):
    in_specs = (P("prow", "pcol"), P(), P(), P())
    out_specs = P("prow", "pcol")
    return jax.shard_map(
        on_device, mesh=mesh, in_specs=in_specs, out_specs=out_specs, check_vma=False
    )
```

```python
import functools

import jax
import jax.numpy as jnp
from jax import lax
from jax.experimental import pallas as pl
from jax.experimental.pallas import tpu as pltpu
from jax.sharding import PartitionSpec as P

NB = 256
ROWS_DEV = 1280
COLS_DEV = 1024
XS = 4
ZS = 4
QUARTER = NB // XS
SUB = QUARTER // ZS
BLOCK = 640
PART = ROWS_DEV // 8
HALF = 32


def shift(core, x, z):
    pairs = []
    for index in range(2 * XS * ZS):
        c, xi, zi = index % 2, index // 2 % XS, index // (2 * XS)
        target = ((zi + z) % ZS * XS + (xi + x) % XS) * 2 + (c + core) % 2
        pairs.append((index, target))
    return pairs


def send(value, core=0, x=0, z=0):
    return lax.ppermute(value, "prow", shift(core, x, z))


def send_from(value, keep, core=0, x=0, z=0):
    pairs = [pair for pair in shift(core, x, z) if keep(pair[0] // 2 % XS, pair[0] // (2 * XS))]
    return lax.ppermute(value, "prow", pairs)


def owned_rows(pivots, prow, number):
    local = pivots.reshape(2 * NB) - prow * ROWS_DEV
    owned = (local >= 0) & (local < ROWS_DEV)
    index = lax.broadcasted_iota(jnp.int32, (2 * NB, 2 * NB), 0)
    other = lax.broadcasted_iota(jnp.int32, (2 * NB, 2 * NB), 1)
    before = jnp.sum(jnp.where(owned[None, :] & (other < index), 1, 0), axis=1)
    slot = jnp.where(owned, before, 2 * NB)
    packed = local * (2 * NB) + number
    entries = jnp.sum(jnp.where(slot[None, :] == index, packed[None, :], 0), axis=1)
    return entries, jnp.sum(jnp.where(owned, 1, 0)).reshape(1)


def pick_kernel(place, entries, count, a_ref, mine, theirs, panel, top, sem, panel_sem, top_sem):
    x, z, core = place[1], place[2], place[3]
    copies = [
        pltpu.make_async_copy(
            a_ref.at[(n % 4 * 2 + n // 4) * PART:(n % 4 * 2 + n // 4 + 1) * PART, :NB],
            panel.at[n * PART:(n + 1) * PART, :],
            panel_sem.at[n],
        )
        for n in range(8)
    ]
    copies.append(pltpu.make_async_copy(a_ref.at[:NB, :], top, top_sem))
    for copy in copies:
        copy.start()
    mine[...] = jnp.zeros_like(mine)
    theirs[...] = jnp.zeros_like(theirs)

    def start(n, carry):
        local, number = entries[n] // (2 * NB), entries[n] % (2 * NB)
        i = number % NB
        quarter, sub, low = i // QUARTER, i // SUB % ZS, i % SUB
        dest = (quarter - x + XS) % XS * QUARTER + (sub - z + ZS) % ZS * SUB + low
        own = core == number // NB
        row = a_ref.at[pl.ds(local, 1), :]

        @pl.when(own)
        def _():
            pltpu.make_async_copy(row, mine.at[pl.ds(dest, 1), :], sem).start()

        @pl.when(jnp.logical_not(own))
        def _():
            pltpu.make_async_copy(row, theirs.at[pl.ds(dest, 1), :], sem).start()

        return carry

    def wait(n, carry):
        pltpu.make_async_copy(a_ref.at[pl.ds(0, 1), :], mine.at[pl.ds(0, 1), :], sem).wait()
        return carry

    lax.fori_loop(0, count[0], start, 0)
    lax.fori_loop(0, count[0], wait, 0)
    for copy in copies:
        copy.wait()


def pick(place, entries, count, matrix):
    smem = pl.BlockSpec(memory_space=pltpu.SMEM)
    vmem = pl.BlockSpec(memory_space=pltpu.VMEM)
    half = jax.ShapeDtypeStruct((NB, COLS_DEV), jnp.float32)
    return pl.pallas_call(
        pick_kernel,
        out_shape=[half, half, jax.ShapeDtypeStruct((ROWS_DEV, NB), jnp.float32), half],
        in_specs=[smem, smem, smem, pl.BlockSpec(memory_space=pltpu.HBM)],
        out_specs=[vmem] * 4,
        scratch_shapes=[
            pltpu.SemaphoreType.DMA, pltpu.SemaphoreType.DMA((8,)), pltpu.SemaphoreType.DMA
        ],
        compiler_params=pltpu.CompilerParams(vmem_limit_bytes=8 * 1024 * 1024),
        name="pick_rows",
    )(place, entries, count, matrix)


def split(value):
    high = value.astype(jnp.bfloat16)
    low = (value - high.astype(jnp.float32)).astype(jnp.bfloat16)
    return high, low


def mul(a, b):
    left = jnp.concatenate([a[0], a[1], a[0]], axis=1)
    right = jnp.concatenate([b[1], b[0], b[0]], axis=0)
    return jnp.dot(left, right, preferred_element_type=jnp.float32)


def three(value):
    high, rest = value.astype(jnp.bfloat16), None
    rest = value - high.astype(jnp.float32)
    middle = rest.astype(jnp.bfloat16)
    return high, middle, (rest - middle.astype(jnp.float32)).astype(jnp.bfloat16)


def spread_kernel(place, own_ref, other_ref, pick_own, pick_other, *refs):
    outs = refs[-XS:]

    @pl.when((place[1] == 0) & (place[2] == 0))
    def _():
        rows = ZS * HALF
        for n in range(COLS_DEV // NB):
            cols = slice(n * NB, (n + 1) * NB)
            own, other = three(own_ref[:, cols]), three(other_ref[:, cols])
            for j in range(XS):
                block = slice(j * rows, (j + 1) * rows)
                dot = functools.partial(jnp.dot, preferred_element_type=jnp.float32)
                total = [
                    dot(pick_own[block, :], a) + dot(pick_other[block, :], b)
                    for a, b in zip(own, other)
                ]
                outs[j][:, cols] = total[0] + (total[1] + total[2])


def spread(place, own, other, picks, tokens):
    smem, vmem = pl.BlockSpec(memory_space=pltpu.SMEM), pl.BlockSpec(memory_space=pltpu.VMEM)
    anywhere = pl.BlockSpec(memory_space=pl.ANY)
    shape = jax.ShapeDtypeStruct((ZS * HALF, COLS_DEV), jnp.float32)
    return pl.pallas_call(
        spread_kernel,
        out_shape=[shape] * XS,
        in_specs=[smem, vmem, vmem, vmem, vmem] + [anywhere] * len(tokens),
        out_specs=[vmem] * XS,
        compiler_params=pltpu.CompilerParams(vmem_limit_bytes=16 * 1024 * 1024),
        name="spread_rows",
    )(place, own, other, *picks, *tokens)


def choose_kernel(axis, tokens, place, *refs):
    pieces, outs = refs[:4], refs[4 + tokens:]
    rows = outs[0].shape[0]
    for n, piece in enumerate(pieces):

        @pl.when(place[axis] == n)
        def _():
            for i, out in enumerate(outs):
                out[...] = piece[i * rows:(i + 1) * rows, :]


def choose(place, axis, pieces, count, tokens):
    smem, vmem = pl.BlockSpec(memory_space=pltpu.SMEM), pl.BlockSpec(memory_space=pltpu.VMEM)
    anywhere = pl.BlockSpec(memory_space=pl.ANY)
    rows, cols = pieces[0].shape
    return pl.pallas_call(
        functools.partial(choose_kernel, axis, len(tokens)),
        out_shape=[jax.ShapeDtypeStruct((rows // count, cols), jnp.float32)] * count,
        in_specs=[smem] + [vmem] * 4 + [anywhere] * len(tokens),
        out_specs=[vmem] * count,
        compiler_params=pltpu.CompilerParams(vmem_limit_bytes=8 * 1024 * 1024),
        name="choose_piece",
    )(place, *pieces, *tokens)


def update_kernel(
    packed, place, entries, count, a_ref, near_ref, far_ref, m_ref, w_ref, *refs
):
    pieces, displaced = refs[:2 * XS], refs[2 * XS:-10]
    out_ref, xs, uh, ul, top, ph, wh, wl, ch, cl = refs[-10:]
    prow, x, z, core, pcol = place[0], place[1], place[2], place[3], place[4]
    block = pl.program_id(0)

    @pl.when(block == 0)
    def _():
        for piece in range(2 * XS):
            step = core if piece < XS else 1 - core
            for k in range(ZS):
                dest = step * NB + (x - piece + 2 * XS) % XS * QUARTER + (z - k + ZS) % ZS * SUB
                dest = pl.multiple_of(dest, SUB)
                xs[pl.ds(dest, SUB), :] = pieces[piece][k * SUB:(k + 1) * SUB, :]
        w0, w1 = split(w_ref[0]), split(w_ref[1])
        wh[0], wl[0] = w0
        wh[1], wl[1] = w1
        m0, m1 = split(m_ref[0]), split(m_ref[1])
        l0r1 = mul(split(xs[NB:, COLS_DEV:]), w0)
        u0c1 = mul(m0, split(xs[:NB, COLS_DEV:]))
        ch[...], cl[...] = split(u0c1)
        l0r1s = split(l0r1)
        u0 = mul(m0, split(xs[:NB, :COLS_DEV]))
        u0s = split(u0)
        uh[:NB, :], ul[:NB, :] = u0s
        y1 = xs[NB:, :COLS_DEV] - mul(l0r1s, u0s)
        u1 = mul(m1, split(y1))
        uh[NB:, :], ul[NB:, :] = split(u1)

        @pl.when(prow == 0)
        def _():
            top[...] = u0

            @pl.when(pcol == 0)
            def _():
                top[:, :NB] = xs[:NB, :NB]

        @pl.when(prow == 1)
        def _():
            top[...] = u1

            @pl.when(pcol == 0)
            def _():
                top[:, :NB] = l0r1

            @pl.when(pcol == 1)
            def _():
                top[:, :NB] = y1[:, :NB]

    out_ref[...] = a_ref[...]
    for y in range(BLOCK // (2 * PART)):
        rows = slice(y * PART, (y + 1) * PART)
        first, second = slice(2 * y * PART, (2 * y + 1) * PART), slice((2 * y + 1) * PART, (2 * y + 2) * PART)

        @pl.when(pcol < 4)
        def _():
            ph[first, :] = near_ref[rows, :]
            ph[second, :] = far_ref[rows, :]

        @pl.when(pcol >= 4)
        def _():
            ph[first, :] = far_ref[rows, :]
            ph[second, :] = near_ref[rows, :]

    base = block * BLOCK

    def patch(n, carry):
        local, number = entries[n] // (2 * NB) - base, entries[n] % (2 * NB)

        @pl.when((local >= 0) & (local < BLOCK))
        def _():
            if packed:
                src = number % HALF
                piece = jnp.where(core == number // HALF, 0, 1)
            else:
                i = number % NB
                src = (z - i // SUB % ZS + ZS) % ZS * SUB + i % SUB
                piece = jnp.where(core == number // NB, 0, XS) + (x - i // QUARTER + XS) % XS
            for j in range(len(displaced)):

                @pl.when(piece == j)
                def _():
                    row = displaced[j][pl.ds(src, 1), :]
                    out_ref[pl.ds(local, 1), :] = row[:, :COLS_DEV]
                    ph[pl.ds(local, 1), :] = row[:, COLS_DEV:]

        return carry

    lax.fori_loop(0, count[0], patch, 0)
    l0 = mul(split(ph[:, :NB]), (wh[0], wl[0]))
    l0s = split(l0)
    l1 = mul(split(ph[:, NB:] - mul(l0s, (ch[...], cl[...]))), (wh[1], wl[1]))
    ls = tuple(jnp.concatenate([a, b], axis=1) for a, b in zip(l0s, split(l1)))
    for n in range(COLS_DEV // NB):
        cols = slice(n * NB, (n + 1) * NB)
        out_ref[:, cols] = out_ref[:, cols] - mul(ls, (uh[:, cols], ul[:, cols]))

    @pl.when(pcol == 0)
    def _():
        out_ref[:, :NB] = l0

    @pl.when(pcol == 1)
    def _():
        out_ref[:, :NB] = l1

    @pl.when((block == 0) & (prow < 2))
    def _():
        out_ref[:NB, :] = top[...]


def update(packed, place, entries, count, matrix, near, far, lower, upper, pieces, displaced):
    smem = pl.BlockSpec(memory_space=pltpu.SMEM)
    vmem = pl.BlockSpec(memory_space=pltpu.VMEM)
    f32, bf16 = jnp.float32, jnp.bfloat16
    wide = pl.BlockSpec((BLOCK, COLS_DEV), lambda i: (i, 0))
    half = pl.BlockSpec((BLOCK // 2, 2 * NB), lambda i: (i, 0))
    return pl.pallas_call(
        functools.partial(update_kernel, packed),
        grid=(ROWS_DEV // BLOCK,),
        out_shape=pltpu.HBM((ROWS_DEV, COLS_DEV), f32),
        in_specs=[smem, smem, smem, wide, half, half]
        + [vmem] * (2 + len(pieces) + len(displaced)),
        out_specs=wide,
        scratch_shapes=[
            pltpu.VMEM((2 * NB, COLS_DEV + NB), f32),
            pltpu.VMEM((2 * NB, COLS_DEV), bf16),
            pltpu.VMEM((2 * NB, COLS_DEV), bf16),
            pltpu.VMEM((NB, COLS_DEV), f32),
            pltpu.VMEM((BLOCK, 2 * NB), f32),
            pltpu.VMEM((2, NB, NB), bf16),
            pltpu.VMEM((2, NB, NB), bf16),
            pltpu.VMEM((NB, NB), bf16),
            pltpu.VMEM((NB, NB), bf16),
        ],
        compiler_params=pltpu.CompilerParams(vmem_limit_bytes=40 * 1024 * 1024),
        name="panel_update",
    )(place, entries, count, matrix, near, far, lower, upper, *pieces, *displaced)


def add_kernel(n, tokens, *refs):
    parts, outs = refs[:n], refs[n + tokens:]
    rows = outs[0].shape[0]
    for i, out in enumerate(outs):
        block = slice(i * rows, (i + 1) * rows)
        value = parts[0][block, :]
        for part in parts[1:]:
            value = value + part[block, :]
        out[...] = value


def add(parts, count, tokens=()):
    vmem, anywhere = pl.BlockSpec(memory_space=pltpu.VMEM), pl.BlockSpec(memory_space=pl.ANY)
    rows, cols = parts[0].shape
    return pl.pallas_call(
        functools.partial(add_kernel, len(parts), len(tokens)),
        out_shape=[jax.ShapeDtypeStruct((rows // count, cols), jnp.float32)] * count,
        in_specs=[vmem] * len(parts) + [anywhere] * len(tokens),
        out_specs=[vmem] * count,
        compiler_params=pltpu.CompilerParams(vmem_limit_bytes=8 * 1024 * 1024),
        name="add_parts",
    )(*parts, *tokens)


def sync(*values):
    anywhere = pl.BlockSpec(memory_space=pl.ANY)
    return pl.pallas_call(
        lambda *refs: None,
        out_shape=[jax.ShapeDtypeStruct(value.shape, value.dtype) for value in values],
        in_specs=[anywhere] * len(values),
        out_specs=[anywhere] * len(values),
        input_output_aliases={i: i for i in range(len(values))},
        compiler_params=pltpu.CompilerParams(vmem_limit_bytes=1024 * 1024),
        name="sync",
    )(*values)


def pack_kernel(groups, count, *refs):
    parts, out = refs[:groups * count], refs[-1]
    col = 0
    for i in range(groups):
        rows, width = parts[i * count].shape
        for k in range(count):
            out[k * rows:(k + 1) * rows, col:col + width] = parts[i * count + k][...]
        col += width


def pack(groups, tokens=()):
    vmem, anywhere = pl.BlockSpec(memory_space=pltpu.VMEM), pl.BlockSpec(memory_space=pl.ANY)
    cols = sum(group[0].shape[1] for group in groups)
    parts = [part for group in groups for part in group]
    return pl.pallas_call(
        functools.partial(pack_kernel, len(groups), len(groups[0])),
        out_shape=jax.ShapeDtypeStruct((groups[0][0].shape[0] * len(groups[0]), cols), jnp.float32),
        in_specs=[vmem] * len(parts) + [anywhere] * len(tokens),
        out_specs=vmem,
        compiler_params=pltpu.CompilerParams(vmem_limit_bytes=8 * 1024 * 1024),
        name="pack_blocks",
    )(*parts, *tokens)


def gather_z(held):
    return [held] + [send(held, z=k) for k in range(1, ZS)]


def gather_x(held):
    pieces = [held] + [send(held, x=j) for j in range(1, XS)]
    return pieces + [send(piece, core=1) for piece in pieces]


def to_columns(value):
    rows = value.shape[0]
    value = lax.all_to_all(jnp.tile(value, (8, 1)), "pcol", 0, 0, tiled=True)
    return value[:rows], value[rows:2 * rows]


def panel_parts(panel):
    parts = lax.all_to_all(panel, "pcol", 0, 0, tiled=True)
    return jnp.concatenate([parts[:PART], parts[PART:2 * PART]], axis=1)


def along_y(parts):
    groups = [[0, 1, 2, 3], [4, 5, 6, 7]]
    return lax.all_to_all(
        jnp.tile(parts, (4, 1)), "pcol", 0, 0, tiled=True, axis_index_groups=groups
    )


def from_root(pieces, axis):
    keep = (lambda xi, zi: xi == 0 and zi == 0) if axis == "x" else (lambda xi, zi: zi == 0)
    return [pieces[0]] + [send_from(pieces[n], keep, **{axis: n}) for n in range(1, 4)]


def on_device(matrix, pivots, lower_inverse, upper_inverse):
    prow = lax.axis_index("prow")
    core, x, z = prow % 2, prow // 2 % XS, prow // (2 * XS)
    place = jnp.stack([prow, x, z, core, lax.axis_index("pcol")]).astype(jnp.int32)
    operands = (place, matrix, pivots, lower_inverse, upper_inverse)
    result, most = exchange(True, *operands)
    return lax.while_loop(
        lambda state: state[0],
        lambda state: (False, exchange(False, *operands)[0]),
        (most >= 2 * HALF, result),
    )[1]


def chip_places(pivots):
    number = lax.broadcasted_iota(jnp.int32, (2 * NB,), 0)
    chip = pivots.reshape(2 * NB) // (2 * ROWS_DEV)
    before = number[None, :] < number[:, None]
    return chip, jnp.sum(jnp.where(before & (chip[None, :] == chip[:, None]), 1, 0), axis=1)


def exchange(packed, place, matrix, pivots, lower_inverse, upper_inverse):
    prow, core = place[0], place[3]

    number = lax.broadcasted_iota(jnp.int32, (2 * NB,), 0)
    entries, count = owned_rows(pivots, prow, number)
    mine, theirs, panel, top = pick(place, entries, count, matrix)
    parts = panel_parts(panel)
    theirs, pivots = sync(theirs, pivots)
    chip, rank = chip_places(pivots)
    summed = add([mine, send(theirs, core=1)], XS)
    received = [send(summed[j], x=j) for j in range(1, XS)]

    if packed:
        other = send_from(top, lambda xi, zi: xi == 0 and zi == 0, core=1)
        where = (chip % XS * ZS + chip // XS) * HALF + rank % HALF
        where = jnp.where(rank // HALF == core, where, -1).reshape(2, 1, NB)
        index = lax.broadcasted_iota(jnp.int32, (XS * ZS * HALF, NB), 0)
        steps = [jnp.where(core == 0, where[k], where[1 - k]) for k in range(2)]
        picks = [(index == step).astype(jnp.bfloat16) for step in steps]
        quarters = spread(place, top, other, picks, summed[:1])
    else:
        quarters = add([top], XS)
    total = add([summed[0]] + received, ZS)
    *total, parts = sync(*total, parts)

    across = lax.ppermute(parts, "pcol", [(n, (n + 4) % 8) for n in range(8)])
    near_rows = along_y(parts)
    received = [send(total[k], z=k) for k in range(1, ZS)]
    total, across, *quarters = sync(add([total[0]] + received, 1)[0], across, *quarters)

    blocks = gather_z(total)
    near_rows, columns = sync(near_rows, total[:, :NB])
    from_0, from_1 = to_columns(columns)
    crossed = jnp.where(core == 0, from_1, from_0)
    subs = choose(place, 1, from_root(quarters, "x"), ZS, [])
    values = sync(*blocks, crossed, across, *subs)
    blocks, crossed, across, subs = values[:ZS], values[ZS], values[ZS + 1], values[ZS + 2:]
    far_rows = along_y(across)

    (displaced,) = choose(place, 2, from_root(subs, "z"), 1, [])
    total, displaced = sync(pack([blocks, gather_z(crossed)]), displaced)

    total = gather_x(total)
    far_rows, columns = sync(far_rows, displaced[:, :NB])
    displaced = pack([[displaced]] + [[part] for part in to_columns(columns)])
    if packed:
        entries, _ = owned_rows(pivots, prow, rank)
        displaced = [displaced, send(displaced, core=1)]
    else:
        displaced = gather_x(pack([gather_z(displaced)]))
    result = update(
        packed, place, entries, count, matrix, near_rows, far_rows, lower_inverse, upper_inverse,
        total, displaced,
    )
    return result, jnp.max(rank)


def solution(mesh):
    in_specs = (P("prow", "pcol"), P(), P(), P())
    out_specs = P("prow", "pcol")
    return jax.shard_map(
        on_device, mesh=mesh, in_specs=in_specs, out_specs=out_specs, check_vma=False
    )
```

```python
import functools

import jax
import jax.numpy as jnp
from jax import lax
from jax.experimental import pallas as pl
from jax.experimental.pallas import tpu as pltpu
from jax.sharding import PartitionSpec as P

NB = 256
ROWS_DEV = 1280
COLS_DEV = 1024
XS = 4
ZS = 4
QUARTER = NB // XS
SUB = QUARTER // ZS
BLOCK = 640
SMALL_BLOCK = 320
PART = ROWS_DEV // 8
HALF = 32


def shift(core, x, z):
    pairs = []
    for index in range(2 * XS * ZS):
        c, xi, zi = index % 2, index // 2 % XS, index // (2 * XS)
        target = ((zi + z) % ZS * XS + (xi + x) % XS) * 2 + (c + core) % 2
        pairs.append((index, target))
    return pairs


def send(value, core=0, x=0, z=0):
    return lax.ppermute(value, "prow", shift(core, x, z))


def send_from(value, keep, core=0, x=0, z=0):
    pairs = [pair for pair in shift(core, x, z) if keep(pair[0] // 2 % XS, pair[0] // (2 * XS))]
    return lax.ppermute(value, "prow", pairs)


def owned_rows(pivots, prow, number):
    local = pivots.reshape(2 * NB) - prow * ROWS_DEV
    owned = (local >= 0) & (local < ROWS_DEV)
    index = lax.broadcasted_iota(jnp.int32, (2 * NB, 2 * NB), 0)
    other = lax.broadcasted_iota(jnp.int32, (2 * NB, 2 * NB), 1)
    before = jnp.sum(jnp.where(owned[None, :] & (other < index), 1, 0), axis=1)
    slot = jnp.where(owned, before, 2 * NB)
    packed = local * (2 * NB) + number
    entries = jnp.sum(jnp.where(slot[None, :] == index, packed[None, :], 0), axis=1)
    return entries, jnp.sum(jnp.where(owned, 1, 0)).reshape(1)


def pick_kernel(place, entries, count, a_ref, mine, theirs, panel, top, sem, panel_sem, top_sem):
    x, z, core = place[1], place[2], place[3]
    copies = [
        pltpu.make_async_copy(
            a_ref.at[(n % 4 * 2 + n // 4) * PART:(n % 4 * 2 + n // 4 + 1) * PART, :NB],
            panel.at[n * PART:(n + 1) * PART, :],
            panel_sem.at[n],
        )
        for n in range(8)
    ]
    copies.append(pltpu.make_async_copy(a_ref.at[:NB, :], top, top_sem))
    for copy in copies:
        copy.start()
    mine[...] = jnp.zeros_like(mine)
    theirs[...] = jnp.zeros_like(theirs)

    def start(n, carry):
        local, number = entries[n] // (2 * NB), entries[n] % (2 * NB)
        i = number % NB
        quarter, sub, low = i // QUARTER, i // SUB % ZS, i % SUB
        dest = (quarter - x + XS) % XS * QUARTER + (sub - z + ZS) % ZS * SUB + low
        own = core == number // NB
        row = a_ref.at[pl.ds(local, 1), :]

        @pl.when(own)
        def _():
            pltpu.make_async_copy(row, mine.at[pl.ds(dest, 1), :], sem).start()

        @pl.when(jnp.logical_not(own))
        def _():
            pltpu.make_async_copy(row, theirs.at[pl.ds(dest, 1), :], sem).start()

        return carry

    def wait(n, carry):
        pltpu.make_async_copy(a_ref.at[pl.ds(0, 1), :], mine.at[pl.ds(0, 1), :], sem).wait()
        return carry

    lax.fori_loop(0, count[0], start, 0)
    lax.fori_loop(0, count[0], wait, 0)
    for copy in copies:
        copy.wait()


def pick(place, entries, count, matrix):
    smem = pl.BlockSpec(memory_space=pltpu.SMEM)
    vmem = pl.BlockSpec(memory_space=pltpu.VMEM)
    half = jax.ShapeDtypeStruct((NB, COLS_DEV), jnp.float32)
    return pl.pallas_call(
        pick_kernel,
        out_shape=[half, half, jax.ShapeDtypeStruct((ROWS_DEV, NB), jnp.float32), half],
        in_specs=[smem, smem, smem, pl.BlockSpec(memory_space=pltpu.HBM)],
        out_specs=[vmem] * 4,
        scratch_shapes=[
            pltpu.SemaphoreType.DMA, pltpu.SemaphoreType.DMA((8,)), pltpu.SemaphoreType.DMA
        ],
        compiler_params=pltpu.CompilerParams(vmem_limit_bytes=8 * 1024 * 1024),
        name="pick_rows",
    )(place, entries, count, matrix)


def split(value):
    high = value.astype(jnp.bfloat16)
    low = (value - high.astype(jnp.float32)).astype(jnp.bfloat16)
    return high, low


def mul(a, b):
    left = jnp.concatenate([a[0], a[1], a[0]], axis=1)
    right = jnp.concatenate([b[1], b[0], b[0]], axis=0)
    return jnp.dot(left, right, preferred_element_type=jnp.float32)


def three(value):
    high, rest = value.astype(jnp.bfloat16), None
    rest = value - high.astype(jnp.float32)
    middle = rest.astype(jnp.bfloat16)
    return high, middle, (rest - middle.astype(jnp.float32)).astype(jnp.bfloat16)


def spread_kernel(place, own_ref, other_ref, pick_own, pick_other, *refs):
    outs = refs[-XS:]

    @pl.when((place[1] == 0) & (place[2] == 0))
    def _():
        rows = ZS * HALF
        for n in range(COLS_DEV // NB):
            cols = slice(n * NB, (n + 1) * NB)
            own, other = three(own_ref[:, cols]), three(other_ref[:, cols])
            for j in range(XS):
                block = slice(j * rows, (j + 1) * rows)
                dot = functools.partial(jnp.dot, preferred_element_type=jnp.float32)
                total = [
                    dot(pick_own[block, :], a) + dot(pick_other[block, :], b)
                    for a, b in zip(own, other)
                ]
                outs[j][:, cols] = total[0] + (total[1] + total[2])


def spread(place, own, other, picks, tokens):
    smem, vmem = pl.BlockSpec(memory_space=pltpu.SMEM), pl.BlockSpec(memory_space=pltpu.VMEM)
    anywhere = pl.BlockSpec(memory_space=pl.ANY)
    shape = jax.ShapeDtypeStruct((ZS * HALF, COLS_DEV), jnp.float32)
    return pl.pallas_call(
        spread_kernel,
        out_shape=[shape] * XS,
        in_specs=[smem, vmem, vmem, vmem, vmem] + [anywhere] * len(tokens),
        out_specs=[vmem] * XS,
        compiler_params=pltpu.CompilerParams(vmem_limit_bytes=16 * 1024 * 1024),
        name="spread_rows",
    )(place, own, other, *picks, *tokens)


def choose_kernel(axis, tokens, place, *refs):
    pieces, outs = refs[:4], refs[4 + tokens:]
    rows = outs[0].shape[0]
    for n, piece in enumerate(pieces):

        @pl.when(place[axis] == n)
        def _():
            for i, out in enumerate(outs):
                out[...] = piece[i * rows:(i + 1) * rows, :]


def choose(place, axis, pieces, count, tokens):
    smem, vmem = pl.BlockSpec(memory_space=pltpu.SMEM), pl.BlockSpec(memory_space=pltpu.VMEM)
    anywhere = pl.BlockSpec(memory_space=pl.ANY)
    rows, cols = pieces[0].shape
    return pl.pallas_call(
        functools.partial(choose_kernel, axis, len(tokens)),
        out_shape=[jax.ShapeDtypeStruct((rows // count, cols), jnp.float32)] * count,
        in_specs=[smem] + [vmem] * 4 + [anywhere] * len(tokens),
        out_specs=[vmem] * count,
        compiler_params=pltpu.CompilerParams(vmem_limit_bytes=8 * 1024 * 1024),
        name="choose_piece",
    )(place, *pieces, *tokens)


def update_kernel(
    packed, place, entries, count, a_ref, near_ref, far_ref, m_ref, w_ref, *refs
):
    pieces, displaced = refs[:2 * XS], refs[2 * XS:-10]
    out_ref, xs, uh, ul, top, ph, wh, wl, ch, cl = refs[-10:]
    prow, x, z, core, pcol = place[0], place[1], place[2], place[3], place[4]
    block, rows_block = pl.program_id(0), BLOCK if packed else SMALL_BLOCK

    @pl.when(block == 0)
    def _():
        for piece in range(2 * XS):
            step = core if piece < XS else 1 - core
            for k in range(ZS):
                dest = step * NB + (x - piece + 2 * XS) % XS * QUARTER + (z - k + ZS) % ZS * SUB
                dest = pl.multiple_of(dest, SUB)
                xs[pl.ds(dest, SUB), :] = pieces[piece][k * SUB:(k + 1) * SUB, :]
        w0, w1 = split(w_ref[0]), split(w_ref[1])
        wh[0], wl[0] = w0
        wh[1], wl[1] = w1
        m0, m1 = split(m_ref[0]), split(m_ref[1])
        l0r1 = mul(split(xs[NB:, COLS_DEV:]), w0)
        u0c1 = mul(m0, split(xs[:NB, COLS_DEV:]))
        ch[...], cl[...] = split(u0c1)
        l0r1s = split(l0r1)

        def upper(n, carry):
            cols = pl.ds(pl.multiple_of(n * width, width), width)
            u0 = mul(m0, split(xs[:NB, cols]))
            u0s = split(u0)
            uh[:NB, cols], ul[:NB, cols] = u0s
            y1 = xs[NB:, cols] - mul(l0r1s, u0s)
            u1 = mul(m1, split(y1))
            uh[NB:, cols], ul[NB:, cols] = split(u1)

            @pl.when(prow == 0)
            def _():
                top[:, cols] = u0

            @pl.when(prow == 1)
            def _():
                top[:, cols] = u1

                @pl.when((pcol == 1) & (n == 0))
                def _():
                    top[:, :NB] = y1[:, :NB]

            return carry

        width = COLS_DEV if packed else NB
        lax.fori_loop(0, COLS_DEV // width, upper, 0)

        @pl.when((prow == 0) & (pcol == 0))
        def _():
            top[:, :NB] = xs[:NB, :NB]

        @pl.when((prow == 1) & (pcol == 0))
        def _():
            top[:, :NB] = l0r1

    out_ref[...] = a_ref[...]
    for y in range(rows_block // (2 * PART)):
        rows = slice(y * PART, (y + 1) * PART)
        first, second = slice(2 * y * PART, (2 * y + 1) * PART), slice((2 * y + 1) * PART, (2 * y + 2) * PART)

        @pl.when(pcol < 4)
        def _():
            ph[first, :] = near_ref[rows, :]
            ph[second, :] = far_ref[rows, :]

        @pl.when(pcol >= 4)
        def _():
            ph[first, :] = far_ref[rows, :]
            ph[second, :] = near_ref[rows, :]

    base = block * rows_block

    def patch(n, carry):
        local, number = entries[n] // (2 * NB) - base, entries[n] % (2 * NB)

        @pl.when((local >= 0) & (local < rows_block))
        def _():
            if packed:
                src = number % HALF
                piece = jnp.where(core == number // HALF, 0, 1)
            else:
                i = number % NB
                src = (z - i // SUB % ZS + ZS) % ZS * SUB + i % SUB
                piece = jnp.where(core == number // NB, 0, XS) + (x - i // QUARTER + XS) % XS
            for j in range(len(displaced)):

                @pl.when(piece == j)
                def _():
                    row = displaced[j][pl.ds(src, 1), :]
                    out_ref[pl.ds(local, 1), :] = row[:, :COLS_DEV]
                    ph[pl.ds(local, 1), :] = row[:, COLS_DEV:]

        return carry

    lax.fori_loop(0, count[0], patch, 0)
    l0 = mul(split(ph[:, :NB]), (wh[0], wl[0]))
    l0s = split(l0)
    l1 = mul(split(ph[:, NB:] - mul(l0s, (ch[...], cl[...]))), (wh[1], wl[1]))
    ls = tuple(jnp.concatenate([a, b], axis=1) for a, b in zip(l0s, split(l1)))

    def subtract(n, carry):
        cols = pl.ds(pl.multiple_of(n * NB, NB), NB)
        out_ref[:, cols] = out_ref[:, cols] - mul(ls, (uh[:, cols], ul[:, cols]))
        return carry

    lax.fori_loop(0, COLS_DEV // NB, subtract, 0, unroll=packed)

    @pl.when(pcol == 0)
    def _():
        out_ref[:, :NB] = l0

    @pl.when(pcol == 1)
    def _():
        out_ref[:, :NB] = l1

    @pl.when((block == 0) & (prow < 2))
    def _():
        out_ref[:NB, :] = top[...]


def update(packed, place, entries, count, matrix, near, far, lower, upper, pieces, displaced):
    smem = pl.BlockSpec(memory_space=pltpu.SMEM)
    vmem = pl.BlockSpec(memory_space=pltpu.VMEM)
    f32, bf16 = jnp.float32, jnp.bfloat16
    rows_block = BLOCK if packed else SMALL_BLOCK
    wide = pl.BlockSpec((rows_block, COLS_DEV), lambda i: (i, 0))
    half = pl.BlockSpec((rows_block // 2, 2 * NB), lambda i: (i, 0))
    return pl.pallas_call(
        functools.partial(update_kernel, packed),
        grid=(ROWS_DEV // rows_block,),
        out_shape=jax.ShapeDtypeStruct((ROWS_DEV, COLS_DEV), f32),
        in_specs=[smem, smem, smem, wide, half, half]
        + [vmem] * (2 + len(pieces) + len(displaced)),
        out_specs=wide,
        scratch_shapes=[
            pltpu.VMEM((2 * NB, COLS_DEV + NB), f32),
            pltpu.VMEM((2 * NB, COLS_DEV), bf16),
            pltpu.VMEM((2 * NB, COLS_DEV), bf16),
            pltpu.VMEM((NB, COLS_DEV), f32),
            pltpu.VMEM((rows_block, 2 * NB), f32),
            pltpu.VMEM((2, NB, NB), bf16),
            pltpu.VMEM((2, NB, NB), bf16),
            pltpu.VMEM((NB, NB), bf16),
            pltpu.VMEM((NB, NB), bf16),
        ],
        compiler_params=pltpu.CompilerParams(vmem_limit_bytes=40 * 1024 * 1024),
        name="panel_update",
    )(place, entries, count, matrix, near, far, lower, upper, *pieces, *displaced)


def add_kernel(n, tokens, *refs):
    parts, outs = refs[:n], refs[n + tokens:]
    rows = outs[0].shape[0]
    for i, out in enumerate(outs):
        block = slice(i * rows, (i + 1) * rows)
        value = parts[0][block, :]
        for part in parts[1:]:
            value = value + part[block, :]
        out[...] = value


def add(parts, count, tokens=()):
    vmem, anywhere = pl.BlockSpec(memory_space=pltpu.VMEM), pl.BlockSpec(memory_space=pl.ANY)
    rows, cols = parts[0].shape
    return pl.pallas_call(
        functools.partial(add_kernel, len(parts), len(tokens)),
        out_shape=[jax.ShapeDtypeStruct((rows // count, cols), jnp.float32)] * count,
        in_specs=[vmem] * len(parts) + [anywhere] * len(tokens),
        out_specs=[vmem] * count,
        compiler_params=pltpu.CompilerParams(vmem_limit_bytes=8 * 1024 * 1024),
        name="add_parts",
    )(*parts, *tokens)


def sync(*values):
    anywhere = pl.BlockSpec(memory_space=pl.ANY)
    return pl.pallas_call(
        lambda *refs: None,
        out_shape=[jax.ShapeDtypeStruct(value.shape, value.dtype) for value in values],
        in_specs=[anywhere] * len(values),
        out_specs=[anywhere] * len(values),
        input_output_aliases={i: i for i in range(len(values))},
        compiler_params=pltpu.CompilerParams(vmem_limit_bytes=1024 * 1024),
        name="sync",
    )(*values)


def pack_kernel(groups, count, *refs):
    parts, out = refs[:groups * count], refs[-1]
    col = 0
    for i in range(groups):
        rows, width = parts[i * count].shape
        for k in range(count):
            out[k * rows:(k + 1) * rows, col:col + width] = parts[i * count + k][...]
        col += width


def pack(groups, tokens=()):
    vmem, anywhere = pl.BlockSpec(memory_space=pltpu.VMEM), pl.BlockSpec(memory_space=pl.ANY)
    cols = sum(group[0].shape[1] for group in groups)
    parts = [part for group in groups for part in group]
    return pl.pallas_call(
        functools.partial(pack_kernel, len(groups), len(groups[0])),
        out_shape=jax.ShapeDtypeStruct((groups[0][0].shape[0] * len(groups[0]), cols), jnp.float32),
        in_specs=[vmem] * len(parts) + [anywhere] * len(tokens),
        out_specs=vmem,
        compiler_params=pltpu.CompilerParams(vmem_limit_bytes=8 * 1024 * 1024),
        name="pack_blocks",
    )(*parts, *tokens)


def gather_z(held):
    return [held] + [send(held, z=k) for k in range(1, ZS)]


def gather_x(held):
    pieces = [held] + [send(held, x=j) for j in range(1, XS)]
    return pieces + [send(piece, core=1) for piece in pieces]


def to_columns(value):
    rows = value.shape[0]
    value = lax.all_to_all(jnp.tile(value, (8, 1)), "pcol", 0, 0, tiled=True)
    return value[:rows], value[rows:2 * rows]


def panel_parts(panel):
    parts = lax.all_to_all(panel, "pcol", 0, 0, tiled=True)
    return jnp.concatenate([parts[:PART], parts[PART:2 * PART]], axis=1)


def along_y(parts):
    groups = [[0, 1, 2, 3], [4, 5, 6, 7]]
    return lax.all_to_all(
        jnp.tile(parts, (4, 1)), "pcol", 0, 0, tiled=True, axis_index_groups=groups
    )


def from_root(pieces, axis):
    keep = (lambda xi, zi: xi == 0 and zi == 0) if axis == "x" else (lambda xi, zi: zi == 0)
    return [pieces[0]] + [send_from(pieces[n], keep, **{axis: n}) for n in range(1, 4)]


def on_device(matrix, pivots, lower_inverse, upper_inverse):
    prow = lax.axis_index("prow")
    core, x, z = prow % 2, prow // 2 % XS, prow // (2 * XS)
    place = jnp.stack([prow, x, z, core, lax.axis_index("pcol")]).astype(jnp.int32)
    operands = (place, matrix, pivots, lower_inverse, upper_inverse)
    result, most = exchange(*operands)
    return lax.while_loop(
        lambda state: state[0],
        lambda state: (False, exchange_all(*operands)),
        (most >= 2 * HALF, result),
    )[1]


def chip_places(pivots):
    number = lax.broadcasted_iota(jnp.int32, (2 * NB,), 0)
    chip = pivots.reshape(2 * NB) // (2 * ROWS_DEV)
    before = number[None, :] < number[:, None]
    return chip, jnp.sum(jnp.where(before & (chip[None, :] == chip[:, None]), 1, 0), axis=1)


def chosen_places(chip, rank, core):
    where = (chip % XS * ZS + chip // XS) * HALF + rank % HALF
    where = jnp.where(rank // HALF == core, where, -1).reshape(2, 1, NB)
    index = lax.broadcasted_iota(jnp.int32, (XS * ZS * HALF, NB), 0)
    steps = [jnp.where(core == 0, where[k], where[1 - k]) for k in range(2)]
    return [(index == step).astype(jnp.bfloat16) for step in steps]


def exchange(place, matrix, pivots, lower_inverse, upper_inverse):
    prow, core = place[0], place[3]

    number = lax.broadcasted_iota(jnp.int32, (2 * NB,), 0)
    entries, count = owned_rows(pivots, prow, number)
    mine, theirs, panel, top = pick(place, entries, count, matrix)
    parts = panel_parts(panel)
    theirs, pivots = sync(theirs, pivots)
    chip, rank = chip_places(pivots)
    summed = add([mine, send(theirs, core=1)], XS)
    received = [send(summed[j], x=j) for j in range(1, XS)]

    other = send_from(top, lambda xi, zi: xi == 0 and zi == 0, core=1)
    picks = chosen_places(chip, rank, core)
    quarters = spread(place, top, other, picks, summed[:1])
    total = add([summed[0]] + received, ZS)
    *total, parts = sync(*total, parts)

    received = [send(total[k], z=k) for k in range(1, ZS)]
    near_rows = along_y(parts)
    across = lax.ppermute(parts, "pcol", [(n, (n + 4) % 8) for n in range(8)])
    total, across, *quarters = sync(add([total[0]] + received, 1)[0], across, *quarters)

    blocks = gather_z(total)
    near_rows, columns = sync(near_rows, total[:, :NB])
    from_0, from_1 = to_columns(columns)
    crossed = jnp.where(core == 0, from_1, from_0)
    subs = choose(place, 1, from_root(quarters, "x"), ZS, [])
    values = sync(*blocks, crossed, across, *subs)
    blocks, crossed, across, subs = values[:ZS], values[ZS], values[ZS + 1], values[ZS + 2:]
    far_rows = along_y(across)

    (displaced,) = choose(place, 2, from_root(subs, "z"), 1, [])
    total, displaced = sync(pack([blocks, gather_z(crossed)]), displaced)

    total = gather_x(total)
    near_rows, far_rows, columns = sync(near_rows, far_rows, displaced[:, :NB])
    displaced = pack([[displaced]] + [[part] for part in to_columns(columns)])
    displaced = [displaced, send(displaced, core=1)]
    entries, _ = owned_rows(pivots, prow, rank)
    result = update(
        True, place, entries, count, matrix, near_rows, far_rows, lower_inverse, upper_inverse,
        total, displaced,
    )
    return result, jnp.max(rank)


def exchange_all(place, matrix, pivots, lower_inverse, upper_inverse):
    prow, x, z, core, pcol = [place[i] for i in range(5)]
    number = lax.broadcasted_iota(jnp.int32, (2 * NB,), 0)
    entries, count = owned_rows(pivots, prow, number)
    mine, theirs, panel, top = pick(place, entries, count, matrix)
    parts = panel_parts(panel)
    panels = lax.all_to_all(jnp.tile(parts, (8, 1)), "pcol", 0, 0, tiled=True)
    panels = panels.reshape(2, 4 * PART, 2 * NB)
    near = pcol < 4
    near_rows = jnp.where(near, panels[0], panels[1])
    far_rows = jnp.where(near, panels[1], panels[0])

    total = add([mine, send(theirs, core=1)], XS)
    total = add([total[0]] + [send(total[j], x=j) for j in range(1, XS)], ZS)
    (total,) = add([total[0]] + [send(total[k], z=k) for k in range(1, ZS)], 1)
    displaced = choose(place, 1, from_root(add([top], XS), "x"), ZS, [])
    (displaced,) = choose(place, 2, from_root(displaced, "z"), 1, [])

    columns = jnp.concatenate([total[:, :NB], displaced[:, :NB]], axis=0)
    from_0, from_1 = to_columns(columns)
    crossed = jnp.where(core == 0, from_1[:SUB], from_0[:SUB])
    held = pack([[total], [crossed], [displaced], [from_0[SUB:]], [from_1[SUB:]]])
    held = pack([gather_z(held)])
    held = pack([[held] + [send(held, x=j) for j in range(1, XS)]])
    both = [held, send(held, core=1)]
    pieces = [h[j * QUARTER:(j + 1) * QUARTER] for h in both for j in range(XS)]
    wide = COLS_DEV + NB
    return update(
        False, place, entries, count, matrix, near_rows, far_rows, lower_inverse, upper_inverse,
        [piece[:, :wide] for piece in pieces], [piece[:, wide:] for piece in pieces],
    )


def solution(mesh):
    in_specs = (P("prow", "pcol"), P(), P(), P())
    out_specs = P("prow", "pcol")
    return jax.shard_map(
        on_device, mesh=mesh, in_specs=in_specs, out_specs=out_specs, check_vma=False
    )
```

```python
import functools

import jax
import jax.numpy as jnp
from jax import lax
from jax.experimental import pallas as pl
from jax.experimental.pallas import tpu as pltpu
from jax.sharding import PartitionSpec as P

NB = 256
ROWS_DEV = 1280
COLS_DEV = 1024
XS = 4
ZS = 4
QUARTER = NB // XS
SUB = QUARTER // ZS
BLOCK = 640
SMALL_BLOCK = 320
PART = ROWS_DEV // 8
HALF = 32


def shift(core, x, z):
    pairs = []
    for index in range(2 * XS * ZS):
        c, xi, zi = index % 2, index // 2 % XS, index // (2 * XS)
        target = ((zi + z) % ZS * XS + (xi + x) % XS) * 2 + (c + core) % 2
        pairs.append((index, target))
    return pairs


def send(value, core=0, x=0, z=0):
    return lax.ppermute(value, "prow", shift(core, x, z))


def send_from(value, keep, core=0, x=0, z=0):
    pairs = [pair for pair in shift(core, x, z) if keep(pair[0] // 2 % XS, pair[0] // (2 * XS))]
    return lax.ppermute(value, "prow", pairs)


def owned_rows(pivots, prow, number):
    local = pivots.reshape(2 * NB) - prow * ROWS_DEV
    owned = (local >= 0) & (local < ROWS_DEV)
    index = lax.broadcasted_iota(jnp.int32, (2 * NB, 2 * NB), 0)
    other = lax.broadcasted_iota(jnp.int32, (2 * NB, 2 * NB), 1)
    before = jnp.sum(jnp.where(owned[None, :] & (other < index), 1, 0), axis=1)
    slot = jnp.where(owned, before, 2 * NB)
    packed = local * (2 * NB) + number
    entries = jnp.sum(jnp.where(slot[None, :] == index, packed[None, :], 0), axis=1)
    return entries, jnp.sum(jnp.where(owned, 1, 0)).reshape(1)


def pick_kernel(place, entries, count, a_ref, mine, theirs, panel, top, sem, panel_sem, top_sem):
    x, z, core = place[1], place[2], place[3]
    copies = [
        pltpu.make_async_copy(
            a_ref.at[(n % 4 * 2 + n // 4) * PART:(n % 4 * 2 + n // 4 + 1) * PART, :NB],
            panel.at[n * PART:(n + 1) * PART, :],
            panel_sem.at[n],
        )
        for n in range(8)
    ]
    copies.append(pltpu.make_async_copy(a_ref.at[:NB, :], top, top_sem))
    for copy in copies:
        copy.start()
    mine[...] = jnp.zeros_like(mine)
    theirs[...] = jnp.zeros_like(theirs)

    def start(n, carry):
        local, number = entries[n] // (2 * NB), entries[n] % (2 * NB)
        i = number % NB
        quarter, sub, low = i // QUARTER, i // SUB % ZS, i % SUB
        dest = (quarter - x + XS) % XS * QUARTER + (sub - z + ZS) % ZS * SUB + low
        own = core == number // NB
        row = a_ref.at[pl.ds(local, 1), :]

        @pl.when(own)
        def _():
            pltpu.make_async_copy(row, mine.at[pl.ds(dest, 1), :], sem).start()

        @pl.when(jnp.logical_not(own))
        def _():
            pltpu.make_async_copy(row, theirs.at[pl.ds(dest, 1), :], sem).start()

        return carry

    def wait(n, carry):
        pltpu.make_async_copy(a_ref.at[pl.ds(0, 1), :], mine.at[pl.ds(0, 1), :], sem).wait()
        return carry

    lax.fori_loop(0, count[0], start, 0)
    lax.fori_loop(0, count[0], wait, 0)
    for copy in copies:
        copy.wait()


def pick(place, entries, count, matrix):
    smem = pl.BlockSpec(memory_space=pltpu.SMEM)
    vmem = pl.BlockSpec(memory_space=pltpu.VMEM)
    half = jax.ShapeDtypeStruct((NB, COLS_DEV), jnp.float32)
    return pl.pallas_call(
        pick_kernel,
        out_shape=[half, half, jax.ShapeDtypeStruct((ROWS_DEV, NB), jnp.float32), half],
        in_specs=[smem, smem, smem, pl.BlockSpec(memory_space=pltpu.HBM)],
        out_specs=[vmem] * 4,
        scratch_shapes=[
            pltpu.SemaphoreType.DMA, pltpu.SemaphoreType.DMA((8,)), pltpu.SemaphoreType.DMA
        ],
        compiler_params=pltpu.CompilerParams(vmem_limit_bytes=8 * 1024 * 1024),
        name="pick_rows",
    )(place, entries, count, matrix)


def split(value):
    high = value.astype(jnp.bfloat16)
    low = (value - high.astype(jnp.float32)).astype(jnp.bfloat16)
    return high, low


def mul(a, b):
    left = jnp.concatenate([a[0], a[1], a[0]], axis=1)
    right = jnp.concatenate([b[1], b[0], b[0]], axis=0)
    return jnp.dot(left, right, preferred_element_type=jnp.float32)


def three(value):
    high, rest = value.astype(jnp.bfloat16), None
    rest = value - high.astype(jnp.float32)
    middle = rest.astype(jnp.bfloat16)
    return high, middle, (rest - middle.astype(jnp.float32)).astype(jnp.bfloat16)


def spread_kernel(place, own_ref, other_ref, pick_own, pick_other, *refs):
    outs = refs[-XS:]

    @pl.when((place[1] == 0) & (place[2] == 0))
    def _():
        rows = ZS * HALF
        for n in range(COLS_DEV // NB):
            cols = slice(n * NB, (n + 1) * NB)
            own, other = three(own_ref[:, cols]), three(other_ref[:, cols])
            for j in range(XS):
                block = slice(j * rows, (j + 1) * rows)
                dot = functools.partial(jnp.dot, preferred_element_type=jnp.float32)
                total = [
                    dot(pick_own[block, :], a) + dot(pick_other[block, :], b)
                    for a, b in zip(own, other)
                ]
                outs[j][:, cols] = total[0] + (total[1] + total[2])


def spread(place, own, other, picks, tokens):
    smem, vmem = pl.BlockSpec(memory_space=pltpu.SMEM), pl.BlockSpec(memory_space=pltpu.VMEM)
    anywhere = pl.BlockSpec(memory_space=pl.ANY)
    shape = jax.ShapeDtypeStruct((ZS * HALF, COLS_DEV), jnp.float32)
    return pl.pallas_call(
        spread_kernel,
        out_shape=[shape] * XS,
        in_specs=[smem, vmem, vmem, vmem, vmem] + [anywhere] * len(tokens),
        out_specs=[vmem] * XS,
        compiler_params=pltpu.CompilerParams(vmem_limit_bytes=16 * 1024 * 1024),
        name="spread_rows",
    )(place, own, other, *picks, *tokens)


def choose_kernel(axis, tokens, place, *refs):
    pieces, outs = refs[:4], refs[4 + tokens:]
    rows = outs[0].shape[0]
    for n, piece in enumerate(pieces):

        @pl.when(place[axis] == n)
        def _():
            for i, out in enumerate(outs):
                out[...] = piece[i * rows:(i + 1) * rows, :]


def choose(place, axis, pieces, count, tokens):
    smem, vmem = pl.BlockSpec(memory_space=pltpu.SMEM), pl.BlockSpec(memory_space=pltpu.VMEM)
    anywhere = pl.BlockSpec(memory_space=pl.ANY)
    rows, cols = pieces[0].shape
    return pl.pallas_call(
        functools.partial(choose_kernel, axis, len(tokens)),
        out_shape=[jax.ShapeDtypeStruct((rows // count, cols), jnp.float32)] * count,
        in_specs=[smem] + [vmem] * 4 + [anywhere] * len(tokens),
        out_specs=[vmem] * count,
        compiler_params=pltpu.CompilerParams(vmem_limit_bytes=8 * 1024 * 1024),
        name="choose_piece",
    )(place, *pieces, *tokens)


def update_kernel(
    packed, place, entries, count, a_ref, near_ref, far_ref, m_ref, w_ref, *refs
):
    pieces, displaced = refs[:2 * XS], refs[2 * XS:-10]
    out_ref, xs, uh, ul, top, ph, wh, wl, ch, cl = refs[-10:]
    prow, x, z, core, pcol = place[0], place[1], place[2], place[3], place[4]
    block, rows_block = pl.program_id(0), BLOCK if packed else SMALL_BLOCK

    @pl.when(block == 0)
    def _():
        for piece in range(2 * XS):
            step = core if piece < XS else 1 - core
            for k in range(ZS):
                dest = step * NB + (x - piece + 2 * XS) % XS * QUARTER + (z - k + ZS) % ZS * SUB
                dest = pl.multiple_of(dest, SUB)
                xs[pl.ds(dest, SUB), :] = pieces[piece][k * SUB:(k + 1) * SUB, :]
        w0, w1 = split(w_ref[0]), split(w_ref[1])
        wh[0], wl[0] = w0
        wh[1], wl[1] = w1
        m0, m1 = split(m_ref[0]), split(m_ref[1])
        l0r1 = mul(split(xs[NB:, COLS_DEV:]), w0)
        u0c1 = mul(m0, split(xs[:NB, COLS_DEV:]))
        ch[...], cl[...] = split(u0c1)
        l0r1s = split(l0r1)

        def upper(n, carry):
            cols = pl.ds(pl.multiple_of(n * width, width), width)
            u0 = mul(m0, split(xs[:NB, cols]))
            u0s = split(u0)
            uh[:NB, cols], ul[:NB, cols] = u0s
            y1 = xs[NB:, cols] - mul(l0r1s, u0s)
            u1 = mul(m1, split(y1))
            uh[NB:, cols], ul[NB:, cols] = split(u1)

            @pl.when(prow == 0)
            def _():
                top[:, cols] = u0

            @pl.when(prow == 1)
            def _():
                top[:, cols] = u1

                @pl.when((pcol == 1) & (n == 0))
                def _():
                    top[:, :NB] = y1[:, :NB]

            return carry

        width = COLS_DEV if packed else NB
        lax.fori_loop(0, COLS_DEV // width, upper, 0)

        @pl.when((prow == 0) & (pcol == 0))
        def _():
            top[:, :NB] = xs[:NB, :NB]

        @pl.when((prow == 1) & (pcol == 0))
        def _():
            top[:, :NB] = l0r1

    out_ref[...] = a_ref[...]
    for y in range(rows_block // (2 * PART)):
        rows = slice(y * PART, (y + 1) * PART)
        first, second = slice(2 * y * PART, (2 * y + 1) * PART), slice((2 * y + 1) * PART, (2 * y + 2) * PART)

        @pl.when(pcol < 4)
        def _():
            ph[first, :] = near_ref[rows, :]
            ph[second, :] = far_ref[rows, :]

        @pl.when(pcol >= 4)
        def _():
            ph[first, :] = far_ref[rows, :]
            ph[second, :] = near_ref[rows, :]

    base = block * rows_block

    def patch(n, carry):
        local, number = entries[n] // (2 * NB) - base, entries[n] % (2 * NB)

        @pl.when((local >= 0) & (local < rows_block))
        def _():
            if packed:
                src = number % HALF
                piece = jnp.where(core == number // HALF, 0, 1)
            else:
                i = number % NB
                src = (z - i // SUB % ZS + ZS) % ZS * SUB + i % SUB
                piece = jnp.where(core == number // NB, 0, XS) + (x - i // QUARTER + XS) % XS
            for j in range(len(displaced)):

                @pl.when(piece == j)
                def _():
                    row = displaced[j][pl.ds(src, 1), :]
                    out_ref[pl.ds(local, 1), :] = row[:, :COLS_DEV]
                    ph[pl.ds(local, 1), :] = row[:, COLS_DEV:]

        return carry

    lax.fori_loop(0, count[0], patch, 0)
    l0 = mul(split(ph[:, :NB]), (wh[0], wl[0]))
    l0s = split(l0)
    l1 = mul(split(ph[:, NB:] - mul(l0s, (ch[...], cl[...]))), (wh[1], wl[1]))
    ls = tuple(jnp.concatenate([a, b], axis=1) for a, b in zip(l0s, split(l1)))

    def subtract(n, carry):
        cols = pl.ds(pl.multiple_of(n * NB, NB), NB)
        out_ref[:, cols] = out_ref[:, cols] - mul(ls, (uh[:, cols], ul[:, cols]))
        return carry

    lax.fori_loop(0, COLS_DEV // NB, subtract, 0, unroll=packed)

    @pl.when(pcol == 0)
    def _():
        out_ref[:, :NB] = l0

    @pl.when(pcol == 1)
    def _():
        out_ref[:, :NB] = l1

    @pl.when((block == 0) & (prow < 2))
    def _():
        out_ref[:NB, :] = top[...]


def update(packed, place, entries, count, matrix, near, far, lower, upper, pieces, displaced):
    smem = pl.BlockSpec(memory_space=pltpu.SMEM)
    vmem = pl.BlockSpec(memory_space=pltpu.VMEM)
    f32, bf16 = jnp.float32, jnp.bfloat16
    rows_block = BLOCK if packed else SMALL_BLOCK
    wide = pl.BlockSpec((rows_block, COLS_DEV), lambda i: (i, 0))
    half = pl.BlockSpec((rows_block // 2, 2 * NB), lambda i: (i, 0))
    return pl.pallas_call(
        functools.partial(update_kernel, packed),
        grid=(ROWS_DEV // rows_block,),
        out_shape=jax.ShapeDtypeStruct((ROWS_DEV, COLS_DEV), f32),
        in_specs=[smem, smem, smem, wide, half, half]
        + [vmem] * (2 + len(pieces) + len(displaced)),
        out_specs=wide,
        scratch_shapes=[
            pltpu.VMEM((2 * NB, COLS_DEV + NB), f32),
            pltpu.VMEM((2 * NB, COLS_DEV), bf16),
            pltpu.VMEM((2 * NB, COLS_DEV), bf16),
            pltpu.VMEM((NB, COLS_DEV), f32),
            pltpu.VMEM((rows_block, 2 * NB), f32),
            pltpu.VMEM((2, NB, NB), bf16),
            pltpu.VMEM((2, NB, NB), bf16),
            pltpu.VMEM((NB, NB), bf16),
            pltpu.VMEM((NB, NB), bf16),
        ],
        compiler_params=pltpu.CompilerParams(vmem_limit_bytes=40 * 1024 * 1024),
        name="panel_update",
    )(place, entries, count, matrix, near, far, lower, upper, *pieces, *displaced)


def add_kernel(n, tokens, *refs):
    parts, outs = refs[:n], refs[n + tokens:]
    rows = outs[0].shape[0]
    for i, out in enumerate(outs):
        block = slice(i * rows, (i + 1) * rows)
        value = parts[0][block, :]
        for part in parts[1:]:
            value = value + part[block, :]
        out[...] = value


def add(parts, count, tokens=()):
    vmem, anywhere = pl.BlockSpec(memory_space=pltpu.VMEM), pl.BlockSpec(memory_space=pl.ANY)
    rows, cols = parts[0].shape
    return pl.pallas_call(
        functools.partial(add_kernel, len(parts), len(tokens)),
        out_shape=[jax.ShapeDtypeStruct((rows // count, cols), jnp.float32)] * count,
        in_specs=[vmem] * len(parts) + [anywhere] * len(tokens),
        out_specs=[vmem] * count,
        compiler_params=pltpu.CompilerParams(vmem_limit_bytes=8 * 1024 * 1024),
        name="add_parts",
    )(*parts, *tokens)


def sync(*values):
    anywhere = pl.BlockSpec(memory_space=pl.ANY)
    return pl.pallas_call(
        lambda *refs: None,
        out_shape=[jax.ShapeDtypeStruct(value.shape, value.dtype) for value in values],
        in_specs=[anywhere] * len(values),
        out_specs=[anywhere] * len(values),
        input_output_aliases={i: i for i in range(len(values))},
        compiler_params=pltpu.CompilerParams(vmem_limit_bytes=1024 * 1024),
        name="sync",
    )(*values)


def pack_kernel(groups, count, *refs):
    parts, out = refs[:groups * count], refs[-1]
    col = 0
    for i in range(groups):
        rows, width = parts[i * count].shape
        for k in range(count):
            out[k * rows:(k + 1) * rows, col:col + width] = parts[i * count + k][...]
        col += width


def pack(groups, tokens=()):
    vmem, anywhere = pl.BlockSpec(memory_space=pltpu.VMEM), pl.BlockSpec(memory_space=pl.ANY)
    cols = sum(group[0].shape[1] for group in groups)
    parts = [part for group in groups for part in group]
    return pl.pallas_call(
        functools.partial(pack_kernel, len(groups), len(groups[0])),
        out_shape=jax.ShapeDtypeStruct((groups[0][0].shape[0] * len(groups[0]), cols), jnp.float32),
        in_specs=[vmem] * len(parts) + [anywhere] * len(tokens),
        out_specs=vmem,
        compiler_params=pltpu.CompilerParams(vmem_limit_bytes=8 * 1024 * 1024),
        name="pack_blocks",
    )(*parts, *tokens)


def gather_z(held):
    return [held] + [send(held, z=k) for k in range(1, ZS)]


def gather_x(held):
    pieces = [held] + [send(held, x=j) for j in range(1, XS)]
    return pieces + [send(piece, core=1) for piece in pieces]


def to_columns(value):
    rows = value.shape[0]
    value = lax.all_to_all(jnp.tile(value, (8, 1)), "pcol", 0, 0, tiled=True)
    return value[:rows], value[rows:2 * rows]


def panel_parts(panel):
    parts = lax.all_to_all(panel, "pcol", 0, 0, tiled=True)
    return jnp.concatenate([parts[:PART], parts[PART:2 * PART]], axis=1)


def along_y(parts):
    groups = [[0, 1, 2, 3], [4, 5, 6, 7]]
    return lax.all_to_all(
        jnp.tile(parts, (4, 1)), "pcol", 0, 0, tiled=True, axis_index_groups=groups
    )


def from_root(pieces, axis):
    keep = (lambda xi, zi: xi == 0 and zi == 0) if axis == "x" else (lambda xi, zi: zi == 0)
    return [pieces[0]] + [send_from(pieces[n], keep, **{axis: n}) for n in range(1, 4)]


def on_device(matrix, pivots, lower_inverse, upper_inverse):
    prow = lax.axis_index("prow")
    core, x, z = prow % 2, prow // 2 % XS, prow // (2 * XS)
    place = jnp.stack([prow, x, z, core, lax.axis_index("pcol")]).astype(jnp.int32)
    operands = (place, matrix, pivots, lower_inverse, upper_inverse)
    result, most = exchange(*operands)
    return lax.while_loop(
        lambda state: state[0],
        lambda state: (False, exchange_all(*operands)),
        (most >= 2 * HALF, result),
    )[1]


def chip_places(pivots):
    number = lax.broadcasted_iota(jnp.int32, (2 * NB,), 0)
    chip = pivots.reshape(2 * NB) // (2 * ROWS_DEV)
    before = number[None, :] < number[:, None]
    return chip, jnp.sum(jnp.where(before & (chip[None, :] == chip[:, None]), 1, 0), axis=1)


def chosen_places(chip, rank, core):
    where = (chip % XS * ZS + chip // XS) * HALF + rank % HALF
    where = jnp.where(rank // HALF == core, where, -1).reshape(2, 1, NB)
    index = lax.broadcasted_iota(jnp.int32, (XS * ZS * HALF, NB), 0)
    steps = [jnp.where(core == 0, where[k], where[1 - k]) for k in range(2)]
    return [(index == step).astype(jnp.bfloat16) for step in steps]


def exchange(place, matrix, pivots, lower_inverse, upper_inverse):
    prow, core = place[0], place[3]

    number = lax.broadcasted_iota(jnp.int32, (2 * NB,), 0)
    entries, count = owned_rows(pivots, prow, number)
    mine, theirs, panel, top = pick(place, entries, count, matrix)
    parts = panel_parts(panel)
    theirs, pivots = sync(theirs, pivots)
    chip, rank = chip_places(pivots)
    summed = add([mine, send(theirs, core=1)], XS)
    received = [send(summed[j], x=j) for j in range(1, XS)]

    other = send_from(top, lambda xi, zi: xi == 0 and zi == 0, core=1)
    picks = chosen_places(chip, rank, core)
    quarters = spread(place, top, other, picks, summed[:1])
    total = add([summed[0]] + received, ZS)
    *total, parts = sync(*total, parts)

    received = [send(total[k], z=k) for k in range(1, ZS)]
    across = lax.ppermute(parts, "pcol", [(n, (n + 4) % 8) for n in range(8)])
    total, across, *quarters = sync(add([total[0]] + received, 1)[0], across, *quarters)

    blocks = gather_z(total)
    from_0, from_1 = to_columns(total[:, :NB])
    crossed = jnp.where(core == 0, from_1, from_0)
    subs = choose(place, 1, from_root(quarters, "x"), ZS, [])
    values = sync(*blocks, crossed, parts, *subs)
    blocks, crossed, parts, subs = values[:ZS], values[ZS], values[ZS + 1], values[ZS + 2:]
    near_rows = along_y(parts)
    far_rows = along_y(across)

    (displaced,) = choose(place, 2, from_root(subs, "z"), 1, [])
    total, displaced = sync(pack([blocks, gather_z(crossed)]), displaced)

    total = gather_x(total)
    near_rows, far_rows, columns = sync(near_rows, far_rows, displaced[:, :NB])
    displaced = pack([[displaced]] + [[part] for part in to_columns(columns)])
    displaced = [displaced, send(displaced, core=1)]
    entries, _ = owned_rows(pivots, prow, rank)
    result = update(
        True, place, entries, count, matrix, near_rows, far_rows, lower_inverse, upper_inverse,
        total, displaced,
    )
    return result, jnp.max(rank)


def exchange_all(place, matrix, pivots, lower_inverse, upper_inverse):
    prow, x, z, core, pcol = [place[i] for i in range(5)]
    number = lax.broadcasted_iota(jnp.int32, (2 * NB,), 0)
    entries, count = owned_rows(pivots, prow, number)
    mine, theirs, panel, top = pick(place, entries, count, matrix)
    parts = panel_parts(panel)
    panels = lax.all_to_all(jnp.tile(parts, (8, 1)), "pcol", 0, 0, tiled=True)
    panels = panels.reshape(2, 4 * PART, 2 * NB)
    near = pcol < 4
    near_rows = jnp.where(near, panels[0], panels[1])
    far_rows = jnp.where(near, panels[1], panels[0])

    total = add([mine, send(theirs, core=1)], XS)
    total = add([total[0]] + [send(total[j], x=j) for j in range(1, XS)], ZS)
    (total,) = add([total[0]] + [send(total[k], z=k) for k in range(1, ZS)], 1)
    displaced = choose(place, 1, from_root(add([top], XS), "x"), ZS, [])
    (displaced,) = choose(place, 2, from_root(displaced, "z"), 1, [])

    columns = jnp.concatenate([total[:, :NB], displaced[:, :NB]], axis=0)
    from_0, from_1 = to_columns(columns)
    crossed = jnp.where(core == 0, from_1[:SUB], from_0[:SUB])
    held = pack([[total], [crossed], [displaced], [from_0[SUB:]], [from_1[SUB:]]])
    held = pack([gather_z(held)])
    held = pack([[held] + [send(held, x=j) for j in range(1, XS)]])
    both = [held, send(held, core=1)]
    pieces = [h[j * QUARTER:(j + 1) * QUARTER] for h in both for j in range(XS)]
    wide = COLS_DEV + NB
    return update(
        False, place, entries, count, matrix, near_rows, far_rows, lower_inverse, upper_inverse,
        [piece[:, :wide] for piece in pieces], [piece[:, wide:] for piece in pieces],
    )


def solution(mesh):
    in_specs = (P("prow", "pcol"), P(), P(), P())
    out_specs = P("prow", "pcol")
    return jax.shard_map(
        on_device, mesh=mesh, in_specs=in_specs, out_specs=out_specs, check_vma=False
    )
```
